32 devices in a mesh: depth: 8 (over z, y), lat: 4 (over x, core).
Axes of the slice: x: 2, y: 2, z: 4, core: 2. Of those that a mesh axis runs over, the one named last changes fastest.
Arguments:
- object_slices: float32 [8, 2, 512, 2048], P('depth', None, 'lat'), as said below
- probe: float32 [2, 2, 256, 256], replicated, may hold values from -2.7 to 2.7
- positions: int32 [16, 2], P('lat'), may hold values from 0 to 1792, as said below
- measured: float32 [16, 256, 256], P('lat'), may hold values from 0 to 0.8
Outputs:
- object_grad: float32 [8, 2, 512, 2048], P('depth', None, 'lat')
The draws below stay inside these ranges and needn't reach their ends.
Inputs may be any that keep to these rules, and one draw needn't show every extreme that they name: Rows 4 l ... 4 l + 3 are the positions of lat index l: their row offset lies in [l * 128, (l + 1) * 128) and their column offset in [0, 1792]. `object_slices`: each cell's magnitude, sqrt(real part squared plus imaginary part squared), lies between 0.9 and 1.
All inputs are finite; a program needn't handle non-finite values.
Results may differ from the reference program's by a relative error of at most 0.039.
Values may be sent and summed in bfloat16 or wider, within the bound.
A program may use at most 64 MiB of HBM per device.

```python
import math
import jax
import jax.numpy as jnp
from jax import lax

PROBE = 256
MODES = 2
POS_DEV = 4
COLS = 2048
TILE = 128
NX = 512
SLICES = 8
POS_TOTAL = 16


def draw_object_slices(key, part):
    mag_key, phase_key = jax.random.split(key)
    shape = (SLICES, NX, COLS)
    magnitude = jax.random.uniform(mag_key, shape, jnp.float32, 0.9, 1.0)
    phase_angle = jax.random.uniform(phase_key, shape, jnp.float32, -0.6, 0.6)
    return jnp.stack([magnitude * jnp.cos(phase_angle), magnitude * jnp.sin(phase_angle)], axis=1)


def draw_positions(key, part):
    row_key, col_key = jax.random.split(key)
    slots = jnp.arange(POS_TOTAL, dtype=jnp.int32)
    owner = slots // POS_DEV
    within = slots % POS_DEV
    spacing = (COLS - PROBE) // POS_DEV
    row_jitter = jax.random.randint(row_key, (POS_TOTAL,), 0, TILE, dtype=jnp.int32)
    col_jitter = jax.random.randint(col_key, (POS_TOTAL,), 0, spacing + 1, dtype=jnp.int32)
    row_offset = owner * TILE + row_jitter
    col_offset = within * spacing + col_jitter
    row_offset = row_offset.at[0].set(0).at[POS_TOTAL - 1].set(NX - 1)
    col_offset = col_offset.at[0].set(0).at[POS_TOTAL - 1].set(COLS - PROBE)
    return jnp.stack([row_offset, col_offset], axis=1).astype(jnp.int32)


def level_of(stream_key, dims, shards, smallest, largest):
    def one(position, parts):
        draws = jax.random.uniform(jax.random.fold_in(jax.random.fold_in(stream_key, 6), position), (parts,), jnp.float32, smallest / len(shards), largest / len(shards))
        return jnp.repeat(jnp.exp(draws), dims[position] // parts).reshape((-1,) + (1,) * (len(dims) - position - 1))

    gain = one(*shards[0])
    for cut in shards[1:]:
        gain = gain * one(*cut)
    return gain


def scatter_about(own_key, dims, deviation, limit, kind=jnp.bfloat16):
    return jnp.clip(deviation * jax.random.normal(own_key, dims, jnp.float32), -limit, limit).astype(kind)


def setup_inputs(seed: int = 0) -> dict:
    keys = jax.random.split(jax.random.key(seed), 5)
    object_slices = draw_object_slices(jax.random.fold_in(keys[4], 71), 0)
    probe = scatter_about(keys[1], (MODES, 2, PROBE, PROBE), 0.45, 2.7, jnp.float32)
    positions = draw_positions(jax.random.fold_in(keys[4], 71), 0)
    measured = jnp.clip(0.8 * jax.random.uniform(keys[3], (POS_TOTAL, PROBE, PROBE), jnp.float32) ** level_of(keys[3], (POS_TOTAL, PROBE, PROBE), ((0, 4),), -0.2, 0.2), 0.0, 0.8)
    return dict(object_slices=object_slices, probe=probe, positions=positions, measured=measured)


fresnel = 0.5

def stack_block(real_part, imag_part):
    return jnp.stack([jnp.stack([real_part, -imag_part]), jnp.stack([imag_part, real_part])]).astype(jnp.float32)

def make_tables(pixels):
    highest = lax.Precision.HIGHEST
    steps_idx = jnp.arange(pixels, dtype=jnp.int32)
    product = steps_idx[:, None] * steps_idx[None, :] % pixels
    angle = 2.0 * math.pi / pixels * product.astype(jnp.float32)
    scale = 1.0 / math.sqrt(pixels)
    d_real = jnp.cos(angle) * scale
    d_imag = -jnp.sin(angle) * scale
    freq = jnp.where(steps_idx < pixels // 2, steps_idx, steps_idx - pixels).astype(jnp.float32)
    theta = math.pi * fresnel / pixels * freq * freq
    h_real = jnp.cos(theta)
    h_imag = -jnp.sin(theta)
    a_real = d_real * h_real[None, :] + d_imag * h_imag[None, :]
    a_imag = d_real * h_imag[None, :] - d_imag * h_real[None, :]
    k_real = jnp.dot(a_real, d_real, precision=highest) - jnp.dot(a_imag, d_imag, precision=highest)
    k_imag = jnp.dot(a_real, d_imag, precision=highest) + jnp.dot(a_imag, d_real, precision=highest)
    return (stack_block(k_real, k_imag), stack_block(k_real.T, -k_imag.T), stack_block(d_real, d_imag), stack_block(d_real, -d_imag))

def transform(table, wave):
    highest = lax.Precision.HIGHEST
    middle = jnp.einsum('srij,mrjk->msik', table, wave.astype(jnp.float32), precision=highest)
    return jnp.einsum('mrik,srlk->msil', middle, table, precision=highest)

def multiply(object_patch, wave_in):
    real_part = object_patch[0] * wave_in[:, 0] - object_patch[1] * wave_in[:, 1]
    imag_part = object_patch[0] * wave_in[:, 1] + object_patch[1] * wave_in[:, 0]
    return jnp.stack([real_part, imag_part], axis=1)

def conj_multiply(object_patch, wave_in):
    real_part = object_patch[0] * wave_in[:, 0] + object_patch[1] * wave_in[:, 1]
    imag_part = object_patch[0] * wave_in[:, 1] - object_patch[1] * wave_in[:, 0]
    return jnp.stack([real_part, imag_part], axis=1)

def conj_sum(wave_in, grad_lit):
    real_part = wave_in[:, 0] * grad_lit[:, 0] + wave_in[:, 1] * grad_lit[:, 1]
    imag_part = wave_in[:, 0] * grad_lit[:, 1] - wave_in[:, 1] * grad_lit[:, 0]
    return jnp.stack([lax.optimization_barrier(jnp.sum(real_part, axis=0)), lax.optimization_barrier(jnp.sum(imag_part, axis=0))])

def reference(object_slices, probe, positions, measured):
    pixels = PROBE
    prop_table, prop_adjoint, far_table, far_adjoint = make_tables(pixels)
    offsets = jnp.arange(pixels, dtype=jnp.int32)

    def one_position(grad_total, inputs):
        place, target = inputs
        rows = ((place[0] + offsets) % NX).astype(jnp.int32)
        cols = (place[1] + offsets).astype(jnp.int32)
        patches = object_slices[:, :, rows[:, None], cols[None, :]]

        def forward(wave_in, patch_block):
            lit_wave = multiply(patch_block, wave_in.astype(jnp.float32))
            return (transform(prop_table, lit_wave).astype(jnp.bfloat16), wave_in)
        last_wave, incidents = lax.scan(forward, probe.astype(jnp.bfloat16), patches)
        far_wave = transform(far_table, last_wave)
        residual = lax.optimization_barrier(jnp.sum(far_wave * far_wave, axis=(0, 1))) - target
        seed_wave = transform(far_adjoint, residual * far_wave).astype(jnp.bfloat16)

        def backward(grad_in, pieces):
            patch_block, in_wave = pieces
            grad_lit = transform(prop_adjoint, grad_in)
            grad_term = conj_sum(in_wave.astype(jnp.float32), grad_lit)
            return (conj_multiply(patch_block, grad_lit).astype(jnp.bfloat16), grad_term)
        _, terms = lax.scan(backward, seed_wave, (patches, incidents), reverse=True)
        grad_total = grad_total.at[:, :, rows[:, None], cols[None, :]].add(terms)
        return (grad_total, None)
    start = jnp.zeros(object_slices.shape, jnp.float32)
    grad_total, _ = lax.scan(one_position, start, (positions, measured))
    return grad_total
```

```python
import functools
import math

import jax
import jax.numpy as jnp
import ml_dtypes
import numpy as np
from jax import lax
from jax.experimental import pallas as pl
from jax.experimental.pallas import tpu as pltpu
from jax.sharding import PartitionSpec as P

fresnel = 0.5
MESH = pl.DeviceIdType.MESH
TILES = 3
LANES = 128
VMEM_BYTES = 48 * 1024 * 1024


def shifted(block, axis, distance):
    devices = range(lax.axis_size(axis))
    route = [((i - distance) % len(devices), i) for i in devices]
    return lax.ppermute(block, axis, route)


def host_tables(pixels):
    idx = np.arange(pixels)
    angle = 2.0 * np.pi * (np.outer(idx, idx) % pixels) / pixels
    far = np.exp(-1j * angle) / math.sqrt(pixels)
    freq = np.where(idx < pixels // 2, idx, idx - pixels).astype(np.float64)
    prop = (np.conj(far) * np.exp(-1j * np.pi * fresnel * freq * freq / pixels)[None, :]) @ far

    def block(table):
        return np.block([[table.real, -table.imag], [table.imag, table.real]])

    prop_block, far_block = block(prop), block(far)
    tables = np.stack([prop_block, prop_block.T, far_block, far_block.T])
    high = tables.astype(ml_dtypes.bfloat16)
    rest = (tables - high.astype(np.float64)).astype(ml_dtypes.bfloat16)
    return jnp.asarray(np.stack([high, rest], axis=1))


def window_place(positions_ref, j, k, tile_rows, col_tiles):
    row = lax.rem(positions_ref[j, k, 0], tile_rows)
    col = positions_ref[j, k, 1]
    first = jnp.minimum(col // LANES, col_tiles - 3)
    return row, first, col - first * LANES


def extract_kernel(positions_ref, tile_ref, blocks_ref):
    _, tile_rows, cols = tile_ref.shape
    _, count, _, _, pixels = blocks_ref.shape
    wide = pixels + LANES

    for j in range(TILES):

        @pl.loop(0, count)
        def _(k):
            row, first, shift = window_place(positions_ref, j, k, tile_rows, cols // LANES)
            start = pl.multiple_of(first * LANES, LANES)
            for part in range(2):
                piece = tile_ref[part, :, pl.ds(start, wide)]
                piece = pltpu.roll(piece, lax.rem(wide - shift, wide), 1)[:, :pixels]
                piece = pltpu.roll(piece, lax.rem(tile_rows - row, tile_rows), 0)
                blocks_ref[j, k, part] = piece.astype(blocks_ref.dtype)


def gather_kernel(positions_ref, terms_ref, grad_ref):
    _, tile_rows, cols = grad_ref.shape
    _, count, _, _, pixels = terms_ref.shape
    wide = pixels + LANES
    grad_ref[...] = jnp.zeros_like(grad_ref)

    for j in range(TILES):

        @pl.loop(0, count)
        def _(k):
            row, first, shift = window_place(positions_ref, j, k, tile_rows, cols // LANES)
            start = pl.multiple_of(first * LANES, LANES)
            for part in range(2):
                piece = terms_ref[j, k, part].astype(jnp.float32)
                piece = pltpu.roll(piece, row, 0)
                piece = jnp.concatenate(
                    [piece, jnp.zeros((tile_rows, LANES), jnp.float32)], axis=1
                )
                piece = pltpu.roll(piece, shift, 1)
                grad_ref[part, :, pl.ds(start, wide)] += piece


def spread(count, sections, lats):
    stride = sections // count
    me = lax.axis_index("depth")
    lat = lax.axis_index("lat")
    works = (lax.rem(me, stride) == lax.rem(lat, stride)) & (me // stride < count)
    return stride, me, lat, works


def worker_of(j, k, lat, lats, stride):
    owner = lax.rem(lat - j + lats, lats)
    return {"depth": k * stride + lax.rem(owner, stride), "lat": owner}


def scatter_kernel(
    count, sections, lats, blocks_ref, held_ref, send_sem, recv_sem, own_sem
):
    stride, me, lat, works = spread(count, sections, lats)
    barrier = pltpu.get_barrier_semaphore()

    @pl.when(works)
    def _():
        for j in range(TILES):
            for s in range(sections):

                @pl.when((s != me) if j == 0 else True)
                def _():
                    pl.semaphore_signal(
                        barrier,
                        inc=1,
                        device_id={"depth": s, "lat": lax.rem(lat + j, lats)},
                        device_id_type=MESH,
                    )

    pl.semaphore_wait(barrier, TILES * count - works.astype(jnp.int32))

    def outgoing(j, k):
        return pltpu.make_async_remote_copy(
            src_ref=blocks_ref.at[j, k],
            dst_ref=held_ref.at[me, j],
            send_sem=send_sem.at[j, k],
            recv_sem=recv_sem.at[me, j],
            device_id=worker_of(j, k, lat, lats, stride),
            device_id_type=MESH,
        )

    def own(k):
        return pltpu.make_async_copy(blocks_ref.at[0, k], held_ref.at[me, 0], own_sem)

    def each(remote, local):
        for j in range(TILES):
            for k in range(count):
                if j == 0:
                    mine = works & (me // stride == k)
                    pl.when(mine)(functools.partial(local, k))
                    pl.when(jnp.logical_not(mine))(functools.partial(remote, j, k))
                else:
                    remote(j, k)

    each(lambda j, k: outgoing(j, k).start(), lambda k: own(k).start())
    each(lambda j, k: outgoing(j, k).wait_send(), lambda k: own(k).wait())

    @pl.when(works)
    def _():
        for j in range(TILES):
            for s in range(sections):

                @pl.when((s != me) if j == 0 else True)
                def _():
                    pltpu.make_async_remote_copy(
                        src_ref=blocks_ref.at[0, 0],
                        dst_ref=held_ref.at[s, j],
                        send_sem=send_sem.at[0, 0],
                        recv_sem=recv_sem.at[s, j],
                        device_id={"depth": s, "lat": lax.rem(lat + j, lats)},
                        device_id_type=MESH,
                    ).wait_recv()


def return_kernel(
    count, sections, lats, made_ref, terms_ref, send_sem, recv_sem, own_sem
):
    stride, me, lat, works = spread(count, sections, lats)
    barrier = pltpu.get_barrier_semaphore()
    my_window = me // stride

    def each(remote, local):
        for j in range(TILES):
            for k in range(count):
                if j == 0:
                    mine = works & (my_window == k)
                    if local is not None:
                        pl.when(mine)(functools.partial(local, k))
                    pl.when(jnp.logical_not(mine))(functools.partial(remote, j, k))
                else:
                    remote(j, k)

    each(
        lambda j, k: pl.semaphore_signal(
            barrier,
            inc=1,
            device_id=worker_of(j, k, lat, lats, stride),
            device_id_type=MESH,
        ),
        None,
    )

    def outgoing(s, j):
        return pltpu.make_async_remote_copy(
            src_ref=made_ref.at[s, j],
            dst_ref=terms_ref.at[j, my_window],
            send_sem=send_sem.at[s, j],
            recv_sem=recv_sem.at[j, my_window],
            device_id={"depth": s, "lat": lax.rem(lat + j, lats)},
            device_id_type=MESH,
        )

    def own():
        return pltpu.make_async_copy(
            made_ref.at[me, 0], terms_ref.at[0, my_window], own_sem
        )

    @pl.when(works)
    def _():
        pl.semaphore_wait(barrier, TILES * sections - 1)
        own().start()
        for wait in (False, True):
            for s in range(sections):
                for j in range(TILES):

                    @pl.when((s != me) if j == 0 else True)
                    def _():
                        copy = outgoing(s, j)
                        copy.wait_send() if wait else copy.start()

        own().wait()

    each(
        lambda j, k: pltpu.make_async_remote_copy(
            src_ref=made_ref.at[0, 0],
            dst_ref=terms_ref.at[j, k],
            send_sem=send_sem.at[0, 0],
            recv_sem=recv_sem.at[j, k],
            device_id=worker_of(j, k, lat, lats, stride),
            device_id_type=MESH,
        ).wait_recv(),
        None,
    )


def transform(left, right, parts, pixels):
    low = jnp.bfloat16
    stacked = jnp.concatenate(
        [jnp.concatenate([p.astype(low) for p in pair], axis=0) for pair in parts], axis=1
    )
    dot = functools.partial(jnp.dot, preferred_element_type=jnp.float32)
    middle = (dot(left[0], stacked) + dot(left[1], stacked)).astype(low)
    rows = [
        jnp.concatenate(
            [
                middle[:pixels, m * pixels : (m + 1) * pixels],
                middle[pixels:, m * pixels : (m + 1) * pixels],
            ],
            axis=1,
        )
        for m in range(len(parts))
    ]
    joined = jnp.concatenate(rows, axis=0)
    ended = dot(joined, right[0]) + dot(joined, right[1])
    return [
        (
            ended[m * pixels : (m + 1) * pixels, :pixels],
            ended[m * pixels : (m + 1) * pixels, pixels:],
        )
        for m in range(len(parts))
    ]


def work_kernel(
    place_ref, held_ref, probe_ref, measured_ref, tables_ref, made_ref, saved, back
):
    sections, _, _, tile_rows, pixels = held_ref.shape
    modes = probe_ref.shape[0]
    keep = tile_rows - place_ref[2]

    def upper():
        return lax.broadcasted_iota(jnp.int32, (tile_rows, pixels), 0) < keep

    def patch(s):
        mask = upper()
        out = []
        for part in range(2):
            a, b, c = (held_ref[s, j, part].astype(jnp.float32) for j in range(TILES))
            out.append(
                jnp.concatenate([jnp.where(mask, a, b), jnp.where(mask, b, c)], axis=0)
            )
        return out

    @pl.when(place_ref[0] == 1)
    def _():
        saved[0] = probe_ref[...].astype(jnp.bfloat16)

        @pl.loop(0, sections)
        def _(s):
            p_real, p_imag = patch(s)
            lit = []
            for m in range(modes):
                w_real = saved[s, m, 0].astype(jnp.float32)
                w_imag = saved[s, m, 1].astype(jnp.float32)
                lit.append(
                    (p_real * w_real - p_imag * w_imag, p_real * w_imag + p_imag * w_real)
                )
            moved = transform(tables_ref[0], tables_ref[1], lit, pixels)
            for m in range(modes):
                for part in range(2):
                    saved[s + 1, m, part] = moved[m][part].astype(jnp.bfloat16)

        last = [(saved[sections, m, 0], saved[sections, m, 1]) for m in range(modes)]
        far = transform(tables_ref[2], tables_ref[3], last, pixels)
        resid = -measured_ref[place_ref[1]]
        for real, imag in far:
            resid = resid + (real * real + imag * imag)
        seed = [(resid * real, resid * imag) for real, imag in far]
        seed = transform(tables_ref[3], tables_ref[2], seed, pixels)
        for m in range(modes):
            for part in range(2):
                back[m, part] = seed[m][part].astype(jnp.bfloat16)

        @pl.loop(0, sections)
        def _(step):
            s = sections - 1 - step
            p_real, p_imag = patch(s)
            waves = [(back[m, 0], back[m, 1]) for m in range(modes)]
            lit = transform(tables_ref[1], tables_ref[0], waves, pixels)
            g_real = jnp.zeros((pixels, pixels), jnp.float32)
            g_imag = jnp.zeros((pixels, pixels), jnp.float32)
            for m in range(modes):
                l_real, l_imag = lit[m]
                w_real = saved[s, m, 0].astype(jnp.float32)
                w_imag = saved[s, m, 1].astype(jnp.float32)
                g_real = g_real + (w_real * l_real + w_imag * l_imag)
                g_imag = g_imag + (w_real * l_imag - w_imag * l_real)
                back[m, 0] = (p_real * l_real + p_imag * l_imag).astype(jnp.bfloat16)
                back[m, 1] = (p_real * l_imag - p_imag * l_real).astype(jnp.bfloat16)
            mask = upper()
            for part, term in enumerate((g_real, g_imag)):
                top, bottom = term[:tile_rows], term[tile_rows:]
                none = jnp.zeros_like(top)
                made_ref[s, 0, part] = jnp.where(mask, top, none).astype(made_ref.dtype)
                made_ref[s, 1, part] = jnp.where(mask, bottom, top).astype(made_ref.dtype)
                made_ref[s, 2, part] = jnp.where(mask, none, bottom).astype(made_ref.dtype)


def on_device(object_slices, probe, positions, measured):
    pixels = probe.shape[-1]
    modes = probe.shape[0]
    tile_rows, cols = object_slices.shape[2:]
    count = positions.shape[0]
    sections = lax.axis_size("depth")
    lats = lax.axis_size("lat")
    stride, me, lat, works = spread(count, sections, lats)
    window = jnp.minimum(me // stride, count - 1)
    low = jnp.bfloat16
    vmem = pl.BlockSpec(memory_space=pltpu.VMEM)
    smem = pl.BlockSpec(memory_space=pltpu.SMEM)
    anywhere = pl.BlockSpec(memory_space=pl.ANY)
    block = (2, tile_rows, pixels)
    local = pltpu.CompilerParams(vmem_limit_bytes=VMEM_BYTES)

    near = jnp.stack([positions] + [shifted(positions, "lat", j) for j in range(1, TILES)])
    own_row = lax.dynamic_index_in_dim(positions, window, 0, False)[0] % tile_rows
    place = jnp.stack([works.astype(jnp.int32), window, own_row]).astype(jnp.int32)

    blocks = pl.pallas_call(
        extract_kernel,
        out_shape=jax.ShapeDtypeStruct((TILES, count) + block, low),
        in_specs=[smem, vmem],
        out_specs=vmem,
        compiler_params=local,
        name="extract",
    )(near, object_slices[0])

    held = pl.pallas_call(
        functools.partial(scatter_kernel, count, sections, lats),
        out_shape=jax.ShapeDtypeStruct((sections, TILES) + block, low),
        in_specs=[anywhere],
        out_specs=anywhere,
        scratch_shapes=[
            pltpu.SemaphoreType.DMA((TILES, count)),
            pltpu.SemaphoreType.DMA((sections, TILES)),
            pltpu.SemaphoreType.DMA,
        ],
        compiler_params=pltpu.CompilerParams(collective_id=0, has_side_effects=True),
        name="scatter",
    )(blocks)

    made = pl.pallas_call(
        work_kernel,
        out_shape=jax.ShapeDtypeStruct((sections, TILES) + block, low),
        in_specs=[smem, vmem, vmem, vmem, vmem],
        out_specs=vmem,
        scratch_shapes=[
            pltpu.VMEM((sections + 1, modes, 2, pixels, pixels), low),
            pltpu.VMEM((modes, 2, pixels, pixels), low),
        ],
        compiler_params=local,
        name="work",
    )(place, held, probe, measured, host_tables(pixels))

    terms = pl.pallas_call(
        functools.partial(return_kernel, count, sections, lats),
        out_shape=jax.ShapeDtypeStruct((TILES, count) + block, low),
        in_specs=[anywhere],
        out_specs=anywhere,
        scratch_shapes=[
            pltpu.SemaphoreType.DMA((sections, TILES)),
            pltpu.SemaphoreType.DMA((TILES, count)),
            pltpu.SemaphoreType.DMA,
        ],
        compiler_params=pltpu.CompilerParams(collective_id=1, has_side_effects=True),
        name="give_back",
    )(made)

    total = pl.pallas_call(
        gather_kernel,
        out_shape=jax.ShapeDtypeStruct((2, tile_rows, cols), jnp.float32),
        in_specs=[smem, vmem],
        out_specs=vmem,
        compiler_params=local,
        name="gather",
    )(near, terms)
    return total[None]


def solution(mesh):
    return jax.shard_map(
        on_device,
        mesh=mesh,
        in_specs=(P("depth", None, "lat", None), P(), P("lat", None), P("lat", None, None)),
        out_specs=P("depth", None, "lat", None),
        check_vma=False,
    )
```

```python
import functools
import math

import jax
import jax.numpy as jnp
import ml_dtypes
import numpy as np
from jax import lax
from jax.experimental import pallas as pl
from jax.experimental.pallas import tpu as pltpu
from jax.sharding import PartitionSpec as P

fresnel = 0.5
MESH = pl.DeviceIdType.MESH
TILES = 3
LANES = 128
VMEM_BYTES = 48 * 1024 * 1024


def shifted(block, axis, distance):
    devices = range(lax.axis_size(axis))
    route = [((i - distance) % len(devices), i) for i in devices]
    return lax.ppermute(block, axis, route)


def host_tables(pixels):
    idx = np.arange(pixels)
    angle = 2.0 * np.pi * (np.outer(idx, idx) % pixels) / pixels
    far = np.exp(-1j * angle) / math.sqrt(pixels)
    freq = np.where(idx < pixels // 2, idx, idx - pixels).astype(np.float64)
    prop = (np.conj(far) * np.exp(-1j * np.pi * fresnel * freq * freq / pixels)[None, :]) @ far

    def block(table):
        return np.block([[table.real, -table.imag], [table.imag, table.real]])

    prop_block, far_block = block(prop), block(far)
    tables = np.stack([prop_block, prop_block.T, far_block, far_block.T])
    high = tables.astype(ml_dtypes.bfloat16)
    rest = (tables - high.astype(np.float64)).astype(ml_dtypes.bfloat16)
    return jnp.asarray(np.stack([high, rest], axis=1))


def window_place(positions_ref, k, tile_rows, col_tiles):
    row = lax.rem(positions_ref[k, 0], tile_rows)
    col = positions_ref[k, 1]
    first = jnp.minimum(col // LANES, col_tiles - 3)
    return row, first, col - first * LANES


def extract_kernel(near0_ref, near1_ref, near2_ref, tile_ref, blocks_ref):
    near = (near0_ref, near1_ref, near2_ref)
    _, _, tile_rows, cols = tile_ref.shape
    _, count, _, _, pixels = blocks_ref.shape
    wide = pixels + LANES

    for j in range(TILES):

        @pl.loop(0, count)
        def _(k):
            row, first, shift = window_place(near[j], k, tile_rows, cols // LANES)
            start = pl.multiple_of(first * LANES, LANES)
            for part in range(2):
                piece = tile_ref[0, part, :, pl.ds(start, wide)]
                piece = pltpu.roll(piece, lax.rem(wide - shift, wide), 1)[:, :pixels]
                piece = pltpu.roll(piece, lax.rem(tile_rows - row, tile_rows), 0)
                blocks_ref[j, k, part] = piece.astype(blocks_ref.dtype)


def gather_kernel(near0_ref, near1_ref, near2_ref, terms_ref, grad_ref):
    near = (near0_ref, near1_ref, near2_ref)
    _, _, tile_rows, cols = grad_ref.shape
    _, count, _, _, pixels = terms_ref.shape
    wide = pixels + LANES
    grad_ref[...] = jnp.zeros_like(grad_ref)

    for j in range(TILES):

        @pl.loop(0, count)
        def _(k):
            row, first, shift = window_place(near[j], k, tile_rows, cols // LANES)
            start = pl.multiple_of(first * LANES, LANES)
            for part in range(2):
                piece = terms_ref[j, k, part].astype(jnp.float32)
                piece = pltpu.roll(piece, row, 0)
                piece = jnp.concatenate(
                    [piece, jnp.zeros((tile_rows, LANES), jnp.float32)], axis=1
                )
                piece = pltpu.roll(piece, shift, 1)
                grad_ref[0, part, :, pl.ds(start, wide)] += piece


def spread(count, sections, lats):
    stride = sections // count
    me = lax.axis_index("depth")
    lat = lax.axis_index("lat")
    works = (lax.rem(me, stride) == lax.rem(lat, stride)) & (me // stride < count)
    return stride, me, lat, works


def worker_of(j, k, lat, lats, stride):
    owner = lax.rem(lat - j + lats, lats)
    return {"depth": k * stride + lax.rem(owner, stride), "lat": owner}


def transform(left, right, parts, pixels):
    low = jnp.bfloat16
    stacked = jnp.concatenate(
        [jnp.concatenate([p.astype(low) for p in pair], axis=0) for pair in parts], axis=1
    )
    dot = functools.partial(jnp.dot, preferred_element_type=jnp.float32)
    middle = (dot(left[0], stacked) + dot(left[1], stacked)).astype(low)
    rows = [
        jnp.concatenate(
            [
                middle[:pixels, m * pixels : (m + 1) * pixels],
                middle[pixels:, m * pixels : (m + 1) * pixels],
            ],
            axis=1,
        )
        for m in range(len(parts))
    ]
    joined = jnp.concatenate(rows, axis=0)
    ended = dot(joined, right[0]) + dot(joined, right[1])
    return [
        (
            ended[m * pixels : (m + 1) * pixels, :pixels],
            ended[m * pixels : (m + 1) * pixels, pixels:],
        )
        for m in range(len(parts))
    ]


def main_kernel(
    count,
    sections,
    lats,
    near0_ref,
    blocks,
    probe_ref,
    measured_ref,
    tables_ref,
    terms_ref,
    held,
    made,
    saved,
    back,
    tables,
    start_wave,
    target,
    load_sem,
    out_sem,
    in_sem,
    own_sem,
    made_sem,
    terms_sem,
):
    tile_rows, pixels = held.shape[3:]
    modes = probe_ref.shape[0]
    stride, me, lat, works = spread(count, sections, lats)
    window = lax.rem(me // stride, count)

    def source(s, j):
        return {"depth": s, "lat": lax.rem(lat + j, lats)}

    def mine(j, k):
        return works & (window == k) if j == 0 else False

    barrier = pltpu.get_barrier_semaphore()
    for j in range(TILES):

        @pl.loop(0, count)
        def _(k):
            @pl.when(jnp.logical_not(mine(j, k)))
            def _():
                pl.semaphore_signal(
                    barrier,
                    inc=1,
                    device_id=worker_of(j, k, lat, lats, stride),
                    device_id_type=MESH,
                )

    loads = (
        pltpu.make_async_copy(tables_ref, tables, load_sem.at[0]),
        pltpu.make_async_copy(probe_ref, start_wave, load_sem.at[1]),
        pltpu.make_async_copy(measured_ref.at[window], target, load_sem.at[2]),
    )

    @pl.when(works)
    def _():
        for j in range(TILES):

            @pl.loop(0, sections)
            def _(s):
                @pl.when((s != me) if j == 0 else True)
                def _():
                    pl.semaphore_signal(
                        barrier, inc=1, device_id=source(s, j), device_id_type=MESH
                    )

        for load in loads:
            load.start()

    busy = works.astype(jnp.int32)
    pl.semaphore_wait(barrier, TILES * count - busy + busy * (TILES * sections - 1))

    def block_out(j, k):
        return pltpu.make_async_remote_copy(
            src_ref=blocks.at[j, k],
            dst_ref=held.at[me, j],
            send_sem=out_sem.at[j, k],
            recv_sem=in_sem.at[me, j],
            device_id=worker_of(j, k, lat, lats, stride),
            device_id_type=MESH,
        )

    def block_own(k):
        return pltpu.make_async_copy(blocks.at[0, k], held.at[me, 0], own_sem.at[0])

    lower_half = 1 - (2 * me) // sections

    @pl.loop(0, count)
    def _(turn):
        k = lower_half * (count - 1 - turn) + (1 - lower_half) * turn
        for j in range(TILES):
            own = mine(j, k)
            if j == 0:

                @pl.when(own)
                def _():
                    block_own(k).start()

            @pl.when(jnp.logical_not(own))
            def _():
                block_out(j, k).start()

    def term_out(s, j):
        return pltpu.make_async_remote_copy(
            src_ref=made.at[s, j],
            dst_ref=terms_ref.at[j, window],
            send_sem=made_sem.at[s, j],
            recv_sem=terms_sem.at[j, window],
            device_id=source(s, j),
            device_id_type=MESH,
        )

    def term_own():
        return pltpu.make_async_copy(
            made.at[me, 0], terms_ref.at[0, window], own_sem.at[1]
        )

    def upper():
        keep = tile_rows - lax.rem(near0_ref[window, 0], tile_rows)
        return lax.broadcasted_iota(jnp.int32, (tile_rows, pixels), 0) < keep

    def patch(s):
        mask = upper()
        out = []
        for part in range(2):
            a, b, c = (held[s, j, part].astype(jnp.float32) for j in range(TILES))
            out.append(
                jnp.concatenate([jnp.where(mask, a, b), jnp.where(mask, b, c)], axis=0)
            )
        return out

    @pl.when(works)
    def _():
        for load in loads:
            load.wait()
        saved[0] = start_wave[...].astype(jnp.bfloat16)
        block_own(window).wait()

        @pl.loop(0, sections)
        def _(s):
            for j in range(TILES):

                @pl.when((s != me) if j == 0 else True)
                def _():
                    pltpu.make_async_remote_copy(
                        src_ref=blocks.at[0, 0],
                        dst_ref=held.at[s, j],
                        send_sem=out_sem.at[0, 0],
                        recv_sem=in_sem.at[s, j],
                        device_id=source(s, j),
                        device_id_type=MESH,
                    ).wait_recv()

            p_real, p_imag = patch(s)
            lit = []
            for m in range(modes):
                w_real = saved[s, m, 0].astype(jnp.float32)
                w_imag = saved[s, m, 1].astype(jnp.float32)
                lit.append(
                    (p_real * w_real - p_imag * w_imag, p_real * w_imag + p_imag * w_real)
                )
            moved = transform(tables.at[0], tables.at[1], lit, pixels)
            for m in range(modes):
                for part in range(2):
                    saved[s + 1, m, part] = moved[m][part].astype(jnp.bfloat16)

        last = [(saved[sections, m, 0], saved[sections, m, 1]) for m in range(modes)]
        far = transform(tables.at[2], tables.at[3], last, pixels)
        resid = -target[...]
        for real, imag in far:
            resid = resid + (real * real + imag * imag)
        seed = [(resid * real, resid * imag) for real, imag in far]
        seed = transform(tables.at[3], tables.at[2], seed, pixels)
        for m in range(modes):
            for part in range(2):
                back[m, part] = seed[m][part].astype(jnp.bfloat16)

        @pl.loop(0, sections)
        def _(step):
            s = sections - 1 - step
            p_real, p_imag = patch(s)
            waves = [(back[m, 0], back[m, 1]) for m in range(modes)]
            lit = transform(tables.at[1], tables.at[0], waves, pixels)
            g_real = jnp.zeros((pixels, pixels), jnp.float32)
            g_imag = jnp.zeros((pixels, pixels), jnp.float32)
            for m in range(modes):
                l_real, l_imag = lit[m]
                w_real = saved[s, m, 0].astype(jnp.float32)
                w_imag = saved[s, m, 1].astype(jnp.float32)
                g_real = g_real + (w_real * l_real + w_imag * l_imag)
                g_imag = g_imag + (w_real * l_imag - w_imag * l_real)
                back[m, 0] = (p_real * l_real + p_imag * l_imag).astype(jnp.bfloat16)
                back[m, 1] = (p_real * l_imag - p_imag * l_real).astype(jnp.bfloat16)
            mask = upper()
            for part, term in enumerate((g_real, g_imag)):
                top, bottom = term[:tile_rows], term[tile_rows:]
                none = jnp.zeros_like(top)
                made[s, 0, part] = jnp.where(mask, top, none).astype(made.dtype)
                made[s, 1, part] = jnp.where(mask, bottom, top).astype(made.dtype)
                made[s, 2, part] = jnp.where(mask, none, bottom).astype(made.dtype)
            for j in range(TILES):

                @pl.when((s != me) if j == 0 else True)
                def _():
                    term_out(s, j).start()

            @pl.when(s == me)
            def _():
                term_own().start()

        @pl.loop(0, sections)
        def _(s):
            for j in range(TILES):

                @pl.when((s != me) if j == 0 else True)
                def _():
                    term_out(s, j).wait_send()

        term_own().wait()

    @pl.loop(0, count)
    def _(k):
        for j in range(TILES):

            @pl.when(jnp.logical_not(mine(j, k)))
            def _():
                block_out(j, k).wait_send()
                pltpu.make_async_remote_copy(
                    src_ref=made.at[0, 0],
                    dst_ref=terms_ref.at[j, k],
                    send_sem=made_sem.at[0, 0],
                    recv_sem=terms_sem.at[j, k],
                    device_id=worker_of(j, k, lat, lats, stride),
                    device_id_type=MESH,
                ).wait_recv()


def on_device(object_slices, probe, positions, measured):
    pixels = probe.shape[-1]
    tile_rows, cols = object_slices.shape[2:]
    count = positions.shape[0]
    sections = lax.axis_size("depth")
    lats = lax.axis_size("lat")
    low = jnp.bfloat16
    vmem = pl.BlockSpec(memory_space=pltpu.VMEM)
    smem = pl.BlockSpec(memory_space=pltpu.SMEM)
    anywhere = pl.BlockSpec(memory_space=pl.ANY)
    block = (2, tile_rows, pixels)
    tables = host_tables(pixels)
    near = [positions] + [shifted(positions, "lat", j) for j in range(1, TILES)]

    blocks = pl.pallas_call(
        extract_kernel,
        out_shape=jax.ShapeDtypeStruct((TILES, count) + block, low),
        in_specs=[smem] * TILES + [vmem],
        out_specs=vmem,
        compiler_params=pltpu.CompilerParams(vmem_limit_bytes=VMEM_BYTES),
        name="extract",
    )(*near, object_slices)

    terms = pl.pallas_call(
        functools.partial(main_kernel, count, sections, lats),
        out_shape=jax.ShapeDtypeStruct((TILES, count) + block, low),
        in_specs=[smem] + [anywhere] * 4,
        out_specs=anywhere,
        scratch_shapes=[
            pltpu.VMEM((sections, TILES) + block, low),
            pltpu.VMEM((sections, TILES) + block, low),
            pltpu.VMEM((sections + 1,) + probe.shape, low),
            pltpu.VMEM(probe.shape, low),
            pltpu.VMEM(tables.shape, low),
            pltpu.VMEM(probe.shape, jnp.float32),
            pltpu.VMEM(measured.shape[1:], jnp.float32),
            pltpu.SemaphoreType.DMA((3,)),
            pltpu.SemaphoreType.DMA((TILES, count)),
            pltpu.SemaphoreType.DMA((sections, TILES)),
            pltpu.SemaphoreType.DMA((2,)),
            pltpu.SemaphoreType.DMA((sections, TILES)),
            pltpu.SemaphoreType.DMA((TILES, count)),
        ],
        compiler_params=pltpu.CompilerParams(
            collective_id=0, has_side_effects=True, vmem_limit_bytes=VMEM_BYTES
        ),
        name="windows",
    )(positions, blocks, probe, measured, tables)

    return pl.pallas_call(
        gather_kernel,
        out_shape=jax.ShapeDtypeStruct(object_slices.shape, jnp.float32),
        in_specs=[smem] * TILES + [vmem],
        out_specs=vmem,
        compiler_params=pltpu.CompilerParams(vmem_limit_bytes=VMEM_BYTES),
        name="gather",
    )(*near, terms)


def solution(mesh):
    return jax.shard_map(
        on_device,
        mesh=mesh,
        in_specs=(P("depth", None, "lat", None), P(), P("lat", None), P("lat", None, None)),
        out_specs=P("depth", None, "lat", None),
        check_vma=False,
    )
```

```python
import functools
import math

import jax
import jax.numpy as jnp
import ml_dtypes
import numpy as np
from jax import lax
from jax.experimental import pallas as pl
from jax.experimental.pallas import tpu as pltpu
from jax.sharding import PartitionSpec as P

fresnel = 0.5
MESH = pl.DeviceIdType.MESH
TILES = 3
SENT = 2
LANES = 128
VMEM_BYTES = 48 * 1024 * 1024


def shifted(block, axis, distance):
    devices = range(lax.axis_size(axis))
    route = [((i - distance) % len(devices), i) for i in devices]
    return lax.ppermute(block, axis, route)


def host_tables(pixels):
    idx = np.arange(pixels)
    angle = 2.0 * np.pi * (np.outer(idx, idx) % pixels) / pixels
    far = np.exp(-1j * angle) / math.sqrt(pixels)
    freq = np.where(idx < pixels // 2, idx, idx - pixels).astype(np.float64)
    prop = (np.conj(far) * np.exp(-1j * np.pi * fresnel * freq * freq / pixels)[None, :]) @ far

    def block(table):
        return np.block([[table.real, -table.imag], [table.imag, table.real]])

    prop_block, far_block = block(prop), block(far)
    tables = np.stack([prop_block, prop_block.T, far_block, far_block.T])
    high = tables.astype(ml_dtypes.bfloat16)
    rest = (tables - high.astype(np.float64)).astype(ml_dtypes.bfloat16)
    return jnp.asarray(np.stack([high, rest], axis=1))


def window_place(positions_ref, k, tile_rows, col_tiles):
    row = lax.rem(positions_ref[k, 0], tile_rows)
    col = positions_ref[k, 1]
    first = jnp.minimum(col // LANES, col_tiles - 3)
    return row, first, col - first * LANES


def upper_rows(shape, keep):
    return lax.broadcasted_iota(jnp.int32, shape, 0) < keep


def extract_kernel(near0_ref, near1_ref, near2_ref, tile_ref, blocks_ref):
    near = (near0_ref, near1_ref, near2_ref)
    _, _, tile_rows, cols = tile_ref.shape
    _, count, _, _, pixels = blocks_ref.shape
    wide = pixels + LANES

    for j in range(TILES):

        @pl.loop(0, count)
        def _(k):
            row, first, shift = window_place(near[j], k, tile_rows, cols // LANES)
            start = pl.multiple_of(first * LANES, LANES)
            for part in range(2):
                piece = tile_ref[0, part, :, pl.ds(start, wide)]
                piece = pltpu.roll(piece, lax.rem(wide - shift, wide), 1)[:, :pixels]
                piece = pltpu.roll(piece, lax.rem(tile_rows - row, tile_rows), 0)
                blocks_ref[j, k, part] = piece.astype(blocks_ref.dtype)


def gather_kernel(near0_ref, near1_ref, near2_ref, terms_ref, grad_ref):
    near = (near0_ref, near1_ref, near2_ref)
    _, _, tile_rows, cols = grad_ref.shape
    _, count, _, _, pixels = terms_ref.shape
    wide = pixels + LANES
    grad_ref[...] = jnp.zeros_like(grad_ref)

    for j in range(TILES):

        @pl.loop(0, count)
        def _(k):
            row, first, shift = window_place(near[j], k, tile_rows, cols // LANES)
            start = pl.multiple_of(first * LANES, LANES)
            for part in range(2):
                piece = terms_ref[j, k, part].astype(jnp.float32)
                if j != 1:
                    upper = upper_rows(piece.shape, tile_rows - row)
                    kept = upper if j == 0 else jnp.logical_not(upper)
                    piece = jnp.where(kept, piece, 0.0)
                piece = pltpu.roll(piece, row, 0)
                piece = jnp.concatenate(
                    [piece, jnp.zeros((tile_rows, LANES), jnp.float32)], axis=1
                )
                piece = pltpu.roll(piece, shift, 1)
                grad_ref[0, part, :, pl.ds(start, wide)] += piece


def spread(count, sections, lats):
    stride = sections // count
    me = lax.axis_index("depth")
    lat = lax.axis_index("lat")
    works = (lax.rem(me, stride) == lax.rem(lat, stride)) & (me // stride < count)
    return stride, me, lat, works


def worker_of(j, k, lat, lats, stride):
    owner = lax.rem(lat - j + lats, lats)
    return {"depth": k * stride + lax.rem(owner, stride), "lat": owner}


def transform(left, right, parts, pixels):
    low = jnp.bfloat16
    stacked = jnp.concatenate(
        [jnp.concatenate([p.astype(low) for p in pair], axis=0) for pair in parts], axis=1
    )
    dot = functools.partial(jnp.dot, preferred_element_type=jnp.float32)
    middle = (dot(left[0], stacked) + dot(left[1], stacked)).astype(low)
    rows = [
        jnp.concatenate(
            [
                middle[:pixels, m * pixels : (m + 1) * pixels],
                middle[pixels:, m * pixels : (m + 1) * pixels],
            ],
            axis=1,
        )
        for m in range(len(parts))
    ]
    joined = jnp.concatenate(rows, axis=0)
    ended = dot(joined, right[0]) + dot(joined, right[1])
    return [
        (
            ended[m * pixels : (m + 1) * pixels, :pixels],
            ended[m * pixels : (m + 1) * pixels, pixels:],
        )
        for m in range(len(parts))
    ]


def main_kernel(
    count,
    sections,
    lats,
    near0_ref,
    blocks,
    probe_ref,
    measured_ref,
    tables_ref,
    terms_ref,
    merged,
    halo,
    held,
    made,
    saved,
    back,
    tables,
    start_wave,
    target,
    load_sem,
    out_sem,
    in_sem,
    own_sem,
    made_sem,
    terms_sem,
    halo_out_sem,
    halo_in_sem,
    pass_sem,
):
    tile_rows, pixels = held.shape[3:]
    modes = probe_ref.shape[0]
    stride, me, lat, works = spread(count, sections, lats)
    window = lax.rem(me // stride, count)

    def source(s, j):
        return {"depth": s, "lat": lax.rem(lat + j, lats)}

    def mine(j, k):
        return works & (window == k) if j == 0 else False

    barrier = pltpu.get_barrier_semaphore()
    for j in range(SENT):

        @pl.loop(0, count)
        def _(k):
            @pl.when(jnp.logical_not(mine(j, k)))
            def _():
                pl.semaphore_signal(
                    barrier,
                    inc=1,
                    device_id=worker_of(j, k, lat, lats, stride),
                    device_id_type=MESH,
                )

    ahead = {"depth": me, "lat": lax.rem(lat + 2, lats)}
    behind = {"depth": me, "lat": lax.rem(lat - 2 + lats, lats)}
    for peer in (ahead, behind):
        pl.semaphore_signal(barrier, inc=1, device_id=peer, device_id_type=MESH)

    loads = (
        pltpu.make_async_copy(tables_ref, tables, load_sem.at[0]),
        pltpu.make_async_copy(probe_ref, start_wave, load_sem.at[1]),
        pltpu.make_async_copy(measured_ref.at[window], target, load_sem.at[2]),
    )

    @pl.when(works)
    def _():
        for j in range(SENT):

            @pl.loop(0, sections)
            def _(s):
                @pl.when((s != me) if j == 0 else True)
                def _():
                    pl.semaphore_signal(
                        barrier, inc=1, device_id=source(s, j), device_id_type=MESH
                    )

        for load in loads:
            load.start()

    busy = works.astype(jnp.int32)
    pl.semaphore_wait(barrier, SENT * count + 2 - busy + busy * (SENT * sections - 1))

    def block_out(j, k):
        return pltpu.make_async_remote_copy(
            src_ref=merged.at[k] if j == 0 else blocks.at[j, k],
            dst_ref=held.at[me, j],
            send_sem=out_sem.at[j, k],
            recv_sem=in_sem.at[me, j],
            device_id=worker_of(j, k, lat, lats, stride),
            device_id_type=MESH,
        )

    def block_own(k):
        return pltpu.make_async_copy(merged.at[k], held.at[me, 0], own_sem.at[0])

    lower_half = 1 - (2 * me) // sections

    def order(turn):
        return lower_half * (count - 1 - turn) + (1 - lower_half) * turn

    def rows_out(k):
        return pltpu.make_async_remote_copy(
            src_ref=blocks.at[2, k],
            dst_ref=halo.at[k],
            send_sem=halo_out_sem.at[k],
            recv_sem=halo_in_sem.at[k],
            device_id=behind,
            device_id_type=MESH,
        )

    @pl.loop(0, count)
    def _(turn):
        rows_out(order(turn)).start()

    @pl.loop(0, count)
    def _(turn):
        block_out(1, order(turn)).start()

    def upper(k):
        keep = tile_rows - lax.rem(near0_ref[k, 0], tile_rows)
        return upper_rows((tile_rows, pixels), keep)

    @pl.loop(0, count)
    def _(turn):
        k = order(turn)
        rows_out(k).wait_recv()
        for part in range(2):
            merged[k, part] = jnp.where(
                upper(k),
                blocks[0, k, part].astype(jnp.float32),
                halo[k, part].astype(jnp.float32),
            ).astype(merged.dtype)
        own = mine(0, k)

        @pl.when(own)
        def _():
            block_own(k).start()

        @pl.when(jnp.logical_not(own))
        def _():
            block_out(0, k).start()

    def term_out(s, j):
        return pltpu.make_async_remote_copy(
            src_ref=made.at[s, j],
            dst_ref=terms_ref.at[j, window],
            send_sem=made_sem.at[s, j],
            recv_sem=terms_sem.at[j, window],
            device_id=source(s, j),
            device_id_type=MESH,
        )

    def term_own():
        return pltpu.make_async_copy(
            made.at[me, 0], terms_ref.at[0, window], own_sem.at[1]
        )

    def patch(s):
        mask = upper(window)
        out = []
        for part in range(2):
            a, b = (held[s, j, part].astype(jnp.float32) for j in range(SENT))
            out.append(
                jnp.concatenate([jnp.where(mask, a, b), jnp.where(mask, b, a)], axis=0)
            )
        return out

    @pl.when(works)
    def _():
        for load in loads:
            load.wait()
        saved[0] = start_wave[...].astype(jnp.bfloat16)
        block_own(window).wait()

        @pl.loop(0, sections)
        def _(s):
            for j in range(SENT):

                @pl.when((s != me) if j == 0 else True)
                def _():
                    pltpu.make_async_remote_copy(
                        src_ref=blocks.at[0, 0],
                        dst_ref=held.at[s, j],
                        send_sem=out_sem.at[0, 0],
                        recv_sem=in_sem.at[s, j],
                        device_id=source(s, j),
                        device_id_type=MESH,
                    ).wait_recv()

            p_real, p_imag = patch(s)
            lit = []
            for m in range(modes):
                w_real = saved[s, m, 0].astype(jnp.float32)
                w_imag = saved[s, m, 1].astype(jnp.float32)
                lit.append(
                    (p_real * w_real - p_imag * w_imag, p_real * w_imag + p_imag * w_real)
                )
            moved = transform(tables.at[0], tables.at[1], lit, pixels)
            for m in range(modes):
                for part in range(2):
                    saved[s + 1, m, part] = moved[m][part].astype(jnp.bfloat16)

        last = [(saved[sections, m, 0], saved[sections, m, 1]) for m in range(modes)]
        far = transform(tables.at[2], tables.at[3], last, pixels)
        resid = -target[...]
        for real, imag in far:
            resid = resid + (real * real + imag * imag)
        seed = [(resid * real, resid * imag) for real, imag in far]
        seed = transform(tables.at[3], tables.at[2], seed, pixels)
        for m in range(modes):
            for part in range(2):
                back[m, part] = seed[m][part].astype(jnp.bfloat16)

        @pl.loop(0, sections)
        def _(step):
            s = sections - 1 - step
            p_real, p_imag = patch(s)
            waves = [(back[m, 0], back[m, 1]) for m in range(modes)]
            lit = transform(tables.at[1], tables.at[0], waves, pixels)
            g_real = jnp.zeros((pixels, pixels), jnp.float32)
            g_imag = jnp.zeros((pixels, pixels), jnp.float32)
            for m in range(modes):
                l_real, l_imag = lit[m]
                w_real = saved[s, m, 0].astype(jnp.float32)
                w_imag = saved[s, m, 1].astype(jnp.float32)
                g_real = g_real + (w_real * l_real + w_imag * l_imag)
                g_imag = g_imag + (w_real * l_imag - w_imag * l_real)
                back[m, 0] = (p_real * l_real + p_imag * l_imag).astype(jnp.bfloat16)
                back[m, 1] = (p_real * l_imag - p_imag * l_real).astype(jnp.bfloat16)
            mask = upper(window)
            for part, term in enumerate((g_real, g_imag)):
                top, bottom = term[:tile_rows], term[tile_rows:]
                made[s, 0, part] = jnp.where(mask, top, bottom).astype(made.dtype)
                made[s, 1, part] = jnp.where(mask, bottom, top).astype(made.dtype)
            for j in range(SENT):

                @pl.when((s != me) if j == 0 else True)
                def _():
                    term_out(s, j).start()

            @pl.when(s == me)
            def _():
                term_own().start()

        term_own().wait()

    def arrived(j, k):
        return pltpu.make_async_remote_copy(
            src_ref=made.at[0, 0],
            dst_ref=terms_ref.at[j, k],
            send_sem=made_sem.at[0, 0],
            recv_sem=terms_sem.at[j, k],
            device_id=worker_of(j, k, lat, lats, stride),
            device_id_type=MESH,
        )

    def pass_on(k):
        return pltpu.make_async_remote_copy(
            src_ref=terms_ref.at[0, k],
            dst_ref=terms_ref.at[2, k],
            send_sem=pass_sem.at[k],
            recv_sem=terms_sem.at[2, k],
            device_id=ahead,
            device_id_type=MESH,
        )

    @pl.loop(0, count)
    def _(turn):
        k = count - 1 - order(turn)

        @pl.when(jnp.logical_not(mine(0, k)))
        def _():
            arrived(0, k).wait_recv()

        pass_on(k).start()

    @pl.when(works)
    def _():
        @pl.loop(0, sections)
        def _(s):
            for j in range(SENT):

                @pl.when((s != me) if j == 0 else True)
                def _():
                    term_out(s, j).wait_send()

    @pl.loop(0, count)
    def _(k):
        rows_out(k).wait_send()
        block_out(1, k).wait_send()
        arrived(1, k).wait_recv()
        pass_on(k).wait()

        @pl.when(jnp.logical_not(mine(0, k)))
        def _():
            block_out(0, k).wait_send()


def on_device(object_slices, probe, positions, measured):
    pixels = probe.shape[-1]
    tile_rows, cols = object_slices.shape[2:]
    count = positions.shape[0]
    sections = lax.axis_size("depth")
    lats = lax.axis_size("lat")
    low = jnp.bfloat16
    vmem = pl.BlockSpec(memory_space=pltpu.VMEM)
    smem = pl.BlockSpec(memory_space=pltpu.SMEM)
    anywhere = pl.BlockSpec(memory_space=pl.ANY)
    block = (2, tile_rows, pixels)
    tables = host_tables(pixels)
    near = [positions] + [shifted(positions, "lat", j) for j in range(1, TILES)]

    blocks = pl.pallas_call(
        extract_kernel,
        out_shape=jax.ShapeDtypeStruct((TILES, count) + block, low),
        in_specs=[smem] * TILES + [vmem],
        out_specs=vmem,
        compiler_params=pltpu.CompilerParams(vmem_limit_bytes=VMEM_BYTES),
        name="extract",
    )(*near, object_slices)

    terms = pl.pallas_call(
        functools.partial(main_kernel, count, sections, lats),
        out_shape=jax.ShapeDtypeStruct((TILES, count) + block, low),
        in_specs=[smem, vmem] + [anywhere] * 3,
        out_specs=anywhere,
        scratch_shapes=[
            pltpu.VMEM((count,) + block, low),
            pltpu.VMEM((count,) + block, low),
            pltpu.VMEM((sections, SENT) + block, low),
            pltpu.VMEM((sections, SENT) + block, low),
            pltpu.VMEM((sections + 1,) + probe.shape, low),
            pltpu.VMEM(probe.shape, low),
            pltpu.VMEM(tables.shape, low),
            pltpu.VMEM(probe.shape, jnp.float32),
            pltpu.VMEM(measured.shape[1:], jnp.float32),
            pltpu.SemaphoreType.DMA((3,)),
            pltpu.SemaphoreType.DMA((SENT, count)),
            pltpu.SemaphoreType.DMA((sections, SENT)),
            pltpu.SemaphoreType.DMA((2,)),
            pltpu.SemaphoreType.DMA((sections, SENT)),
            pltpu.SemaphoreType.DMA((TILES, count)),
            pltpu.SemaphoreType.DMA((count,)),
            pltpu.SemaphoreType.DMA((count,)),
            pltpu.SemaphoreType.DMA((count,)),
        ],
        compiler_params=pltpu.CompilerParams(
            collective_id=0, has_side_effects=True, vmem_limit_bytes=VMEM_BYTES
        ),
        name="windows",
    )(positions, blocks, probe, measured, tables)

    return pl.pallas_call(
        gather_kernel,
        out_shape=jax.ShapeDtypeStruct(object_slices.shape, jnp.float32),
        in_specs=[smem] * TILES + [vmem],
        out_specs=vmem,
        compiler_params=pltpu.CompilerParams(vmem_limit_bytes=VMEM_BYTES),
        name="gather",
    )(*near, terms)


def solution(mesh):
    return jax.shard_map(
        on_device,
        mesh=mesh,
        in_specs=(P("depth", None, "lat", None), P(), P("lat", None), P("lat", None, None)),
        out_specs=P("depth", None, "lat", None),
        check_vma=False,
    )
```

```python
import functools
import math

import jax
import jax.numpy as jnp
import ml_dtypes
import numpy as np
from jax import lax
from jax.experimental import pallas as pl
from jax.experimental.pallas import tpu as pltpu
from jax.sharding import PartitionSpec as P

fresnel = 0.5
MESH = pl.DeviceIdType.MESH
TILES = 3
SENT = 2
LANES = 128
VMEM_BYTES = 48 * 1024 * 1024


def shifted(block, axis, distance):
    devices = range(lax.axis_size(axis))
    route = [((i - distance) % len(devices), i) for i in devices]
    return lax.ppermute(block, axis, route)


def host_tables(pixels):
    idx = np.arange(pixels)
    angle = 2.0 * np.pi * (np.outer(idx, idx) % pixels) / pixels
    far = np.exp(-1j * angle) / math.sqrt(pixels)
    freq = np.where(idx < pixels // 2, idx, idx - pixels).astype(np.float64)
    prop = (np.conj(far) * np.exp(-1j * np.pi * fresnel * freq * freq / pixels)[None, :]) @ far

    def block(table):
        return np.block([[table.real, -table.imag], [table.imag, table.real]])

    prop_block, far_block = block(prop), block(far)
    tables = np.stack([prop_block, prop_block.T, far_block, far_block.T])
    high = tables.astype(ml_dtypes.bfloat16)
    rest = (tables - high.astype(np.float64)).astype(ml_dtypes.bfloat16)
    return jnp.asarray(np.stack([high, rest], axis=1))


def window_place(positions_ref, k, tile_rows, col_tiles):
    row = lax.rem(positions_ref[k, 0], tile_rows)
    col = positions_ref[k, 1]
    first = jnp.minimum(col // LANES, col_tiles - 3)
    return row, first, col - first * LANES


def upper_rows(shape, keep):
    return lax.broadcasted_iota(jnp.int32, shape, 0) < keep


def extract_kernel(near0_ref, near1_ref, near2_ref, tile_ref, blocks_ref):
    near = (near0_ref, near1_ref, near2_ref)
    _, _, tile_rows, cols = tile_ref.shape
    _, count, _, _, pixels = blocks_ref.shape
    wide = pixels + LANES

    for j in range(TILES):

        @pl.loop(0, count)
        def _(k):
            row, first, shift = window_place(near[j], k, tile_rows, cols // LANES)
            start = pl.multiple_of(first * LANES, LANES)
            for part in range(2):
                piece = tile_ref[0, part, :, pl.ds(start, wide)]
                piece = pltpu.roll(piece, lax.rem(wide - shift, wide), 1)[:, :pixels]
                piece = pltpu.roll(piece, lax.rem(tile_rows - row, tile_rows), 0)
                blocks_ref[j, k, part] = piece.astype(blocks_ref.dtype)


def gather_kernel(near0_ref, near1_ref, near2_ref, terms_ref, grad_ref):
    near = (near0_ref, near1_ref, near2_ref)
    _, _, tile_rows, cols = grad_ref.shape
    _, count, _, _, pixels = terms_ref.shape
    wide = pixels + LANES
    grad_ref[...] = jnp.zeros_like(grad_ref)

    for j in range(TILES):

        @pl.loop(0, count)
        def _(k):
            row, first, shift = window_place(near[j], k, tile_rows, cols // LANES)
            start = pl.multiple_of(first * LANES, LANES)
            for part in range(2):
                piece = terms_ref[j, k, part].astype(jnp.float32)
                if j != 1:
                    upper = upper_rows(piece.shape, tile_rows - row)
                    kept = upper if j == 0 else jnp.logical_not(upper)
                    piece = jnp.where(kept, piece, 0.0)
                piece = pltpu.roll(piece, row, 0)
                piece = jnp.concatenate(
                    [piece, jnp.zeros((tile_rows, LANES), jnp.float32)], axis=1
                )
                piece = pltpu.roll(piece, shift, 1)
                grad_ref[0, part, :, pl.ds(start, wide)] += piece


def spread(count, sections, lats):
    stride = sections // count
    me = lax.axis_index("depth")
    lat = lax.axis_index("lat")
    works = (lax.rem(me, stride) == lax.rem(lat, stride)) & (me // stride < count)
    return stride, me, lat, works


def worker_of(j, k, lat, lats, stride):
    owner = lax.rem(lat - j + lats, lats)
    return {"depth": k * stride + lax.rem(owner, stride), "lat": owner}


def transform(left, right, parts, pixels):
    low = jnp.bfloat16
    stacked = jnp.concatenate(
        [jnp.concatenate([p.astype(low) for p in pair], axis=0) for pair in parts], axis=1
    )
    dot = functools.partial(jnp.dot, preferred_element_type=jnp.float32)
    middle = (dot(left[0], stacked) + dot(left[1], stacked)).astype(low)
    rows = [
        jnp.concatenate(
            [
                middle[:pixels, m * pixels : (m + 1) * pixels],
                middle[pixels:, m * pixels : (m + 1) * pixels],
            ],
            axis=1,
        )
        for m in range(len(parts))
    ]
    joined = jnp.concatenate(rows, axis=0)
    ended = dot(joined, right[0]) + dot(joined, right[1])
    return [
        (
            ended[m * pixels : (m + 1) * pixels, :pixels],
            ended[m * pixels : (m + 1) * pixels, pixels:],
        )
        for m in range(len(parts))
    ]


def main_kernel(
    count,
    sections,
    lats,
    near0_ref,
    blocks,
    probe_ref,
    measured_ref,
    tables_ref,
    terms_ref,
    merged,
    halo,
    held,
    made,
    whole,
    side,
    grads,
    power,
    saved,
    back,
    tables,
    start_wave,
    target,
    load_sem,
    out_sem,
    in_sem,
    own_sem,
    made_sem,
    terms_sem,
    halo_out_sem,
    halo_in_sem,
    pass_sem,
    whole_out_sem,
    whole_in_sem,
    side_out_sem,
    side_in_sem,
    power_sem,
):
    tile_rows, pixels = held.shape[3:]
    modes = start_wave.shape[0]
    stride, me, lat, works = spread(count, sections, lats)
    window = lax.rem(me // stride, count)
    pair_lat = lat + 1 - 2 * lax.rem(lat, 2)
    pair = {"depth": me, "lat": pair_lat}
    helps = (lax.rem(me, stride) == lax.rem(pair_lat, stride)) & (me // stride < count)
    lead, helper = works.astype(jnp.int32), helps.astype(jnp.int32)

    def source(s, j):
        return {"depth": s, "lat": lax.rem(lat + j, lats)}

    def mine(j, k):
        return works & (window == k) if j == 0 else False

    barrier = pltpu.get_barrier_semaphore()
    for j in range(SENT):

        @pl.loop(0, count)
        def _(k):
            @pl.when(jnp.logical_not(mine(j, k)))
            def _():
                pl.semaphore_signal(
                    barrier,
                    inc=1,
                    device_id=worker_of(j, k, lat, lats, stride),
                    device_id_type=MESH,
                )

    ahead = {"depth": me, "lat": lax.rem(lat + 2, lats)}
    behind = {"depth": me, "lat": lax.rem(lat - 2 + lats, lats)}
    for peer in (ahead, behind):
        pl.semaphore_signal(barrier, inc=1, device_id=peer, device_id_type=MESH)

    loads = (
        pltpu.make_async_copy(tables_ref, tables, load_sem.at[0]),
        pltpu.make_async_copy(
            probe_ref.at[pl.ds(helper * modes, modes)], start_wave, load_sem.at[1]
        ),
        pltpu.make_async_copy(measured_ref.at[window], target, load_sem.at[2]),
    )

    @pl.when(works)
    def _():
        for j in range(SENT):

            @pl.loop(0, sections)
            def _(s):
                @pl.when((s != me) if j == 0 else True)
                def _():
                    pl.semaphore_signal(
                        barrier, inc=1, device_id=source(s, j), device_id_type=MESH
                    )

    @pl.when(works | helps)
    def _():
        pl.semaphore_signal(barrier, inc=1, device_id=pair, device_id_type=MESH)
        for load in loads:
            load.start()

    pl.semaphore_wait(barrier, SENT * count + 2 + lead * (SENT * sections - 1) + helper)

    def block_out(j, k):
        return pltpu.make_async_remote_copy(
            src_ref=merged.at[k] if j == 0 else blocks.at[j, k],
            dst_ref=held.at[me, j],
            send_sem=out_sem.at[j, k],
            recv_sem=in_sem.at[me, j],
            device_id=worker_of(j, k, lat, lats, stride),
            device_id_type=MESH,
        )

    def block_own(k):
        return pltpu.make_async_copy(merged.at[k], held.at[me, 0], own_sem.at[0])

    lower_half = 1 - (2 * me) // sections

    def order(turn):
        return lower_half * (count - 1 - turn) + (1 - lower_half) * turn

    def rows_out(k):
        return pltpu.make_async_remote_copy(
            src_ref=blocks.at[2, k],
            dst_ref=halo.at[k],
            send_sem=halo_out_sem.at[k],
            recv_sem=halo_in_sem.at[k],
            device_id=behind,
            device_id_type=MESH,
        )

    @pl.loop(0, count)
    def _(turn):
        rows_out(order(turn)).start()

    @pl.loop(0, count)
    def _(turn):
        block_out(1, order(turn)).start()

    def upper(k):
        keep = tile_rows - lax.rem(near0_ref[k, 0], tile_rows)
        return upper_rows((tile_rows, pixels), keep)

    @pl.loop(0, count)
    def _(turn):
        k = order(turn)
        rows_out(k).wait_recv()
        for part in range(2):
            merged[k, part] = jnp.where(
                upper(k),
                blocks[0, k, part].astype(jnp.float32),
                halo[k, part].astype(jnp.float32),
            ).astype(merged.dtype)
        own = mine(0, k)

        @pl.when(own)
        def _():
            block_own(k).start()

        @pl.when(jnp.logical_not(own))
        def _():
            block_out(0, k).start()

    def term_out(s, j):
        return pltpu.make_async_remote_copy(
            src_ref=made.at[s, j],
            dst_ref=terms_ref.at[j, window],
            send_sem=made_sem.at[s, j],
            recv_sem=terms_sem.at[j, window],
            device_id=source(s, j),
            device_id_type=MESH,
        )

    def term_own():
        return pltpu.make_async_copy(
            made.at[me, 0], terms_ref.at[0, window], own_sem.at[1]
        )

    def whole_out(s):
        return pltpu.make_async_remote_copy(
            src_ref=whole.at[s],
            dst_ref=whole.at[s],
            send_sem=whole_out_sem.at[s],
            recv_sem=whole_in_sem.at[s],
            device_id=pair,
            device_id_type=MESH,
        )

    def side_out(s):
        return pltpu.make_async_remote_copy(
            src_ref=side.at[s],
            dst_ref=side.at[s],
            send_sem=side_out_sem.at[s],
            recv_sem=side_in_sem.at[s],
            device_id=pair,
            device_id_type=MESH,
        )

    def power_out():
        return pltpu.make_async_remote_copy(
            src_ref=power.at[0],
            dst_ref=power.at[1],
            send_sem=power_sem.at[0],
            recv_sem=power_sem.at[1],
            device_id=pair,
            device_id_type=MESH,
        )

    def assemble(s):
        for j in range(SENT):

            @pl.when((s != me) if j == 0 else True)
            def _():
                pltpu.make_async_remote_copy(
                    src_ref=blocks.at[0, 0],
                    dst_ref=held.at[s, j],
                    send_sem=out_sem.at[0, 0],
                    recv_sem=in_sem.at[s, j],
                    device_id=source(s, j),
                    device_id_type=MESH,
                ).wait_recv()

        mask = upper(window)
        for part in range(2):
            a, b = (held[s, j, part].astype(jnp.float32) for j in range(SENT))
            whole[s, part, :tile_rows] = jnp.where(mask, a, b).astype(whole.dtype)
            whole[s, part, tile_rows:] = jnp.where(mask, b, a).astype(whole.dtype)
        whole_out(s).start()

    def finish(s):
        side_out(s).wait_recv()
        mask = upper(window)
        for part in range(2):
            term = grads[lax.rem(s, 2), part] + side[s, part].astype(jnp.float32)
            top, bottom = term[:tile_rows], term[tile_rows:]
            made[s, 0, part] = jnp.where(mask, top, bottom).astype(made.dtype)
            made[s, 1, part] = jnp.where(mask, bottom, top).astype(made.dtype)
        for j in range(SENT):

            @pl.when((s != me) if j == 0 else True)
            def _():
                term_out(s, j).start()

        @pl.when(s == me)
        def _():
            term_own().start()

    @pl.when(works)
    def _():
        block_own(window).wait()

    @pl.when(works | helps)
    def _():
        for load in loads:
            load.wait()
        saved[0] = start_wave[...].astype(jnp.bfloat16)

        @pl.loop(0, sections)
        def _(s):
            @pl.when(works)
            def _():
                assemble(s)

            @pl.when(helps)
            def _():
                whole_out(s).wait_recv()

            p_real, p_imag = (whole[s, part].astype(jnp.float32) for part in range(2))
            lit = []
            for m in range(modes):
                w_real = saved[s, m, 0].astype(jnp.float32)
                w_imag = saved[s, m, 1].astype(jnp.float32)
                lit.append(
                    (p_real * w_real - p_imag * w_imag, p_real * w_imag + p_imag * w_real)
                )
            moved = transform(tables.at[0], tables.at[1], lit, pixels)
            for m in range(modes):
                for part in range(2):
                    saved[s + 1, m, part] = moved[m][part].astype(jnp.bfloat16)

        last = [(saved[sections, m, 0], saved[sections, m, 1]) for m in range(modes)]
        far = transform(tables.at[2], tables.at[3], last, pixels)
        power[0] = sum(real * real + imag * imag for real, imag in far)

        @pl.when(works)
        def _():
            power[0] = power[0] - target[...]

        power_out().start()
        power_out().wait()
        resid = power[0] + power[1]
        seed = [(resid * real, resid * imag) for real, imag in far]
        seed = transform(tables.at[3], tables.at[2], seed, pixels)
        for m in range(modes):
            for part in range(2):
                back[m, part] = seed[m][part].astype(jnp.bfloat16)

        @pl.loop(0, sections)
        def _(step):
            s = sections - 1 - step
            p_real, p_imag = (whole[s, part].astype(jnp.float32) for part in range(2))
            waves = [(back[m, 0], back[m, 1]) for m in range(modes)]
            lit = transform(tables.at[1], tables.at[0], waves, pixels)
            g_real = jnp.zeros((pixels, pixels), jnp.float32)
            g_imag = jnp.zeros((pixels, pixels), jnp.float32)
            for m in range(modes):
                l_real, l_imag = lit[m]
                w_real = saved[s, m, 0].astype(jnp.float32)
                w_imag = saved[s, m, 1].astype(jnp.float32)
                g_real = g_real + (w_real * l_real + w_imag * l_imag)
                g_imag = g_imag + (w_real * l_imag - w_imag * l_real)
                back[m, 0] = (p_real * l_real + p_imag * l_imag).astype(jnp.bfloat16)
                back[m, 1] = (p_real * l_imag - p_imag * l_real).astype(jnp.bfloat16)

            @pl.when(works)
            def _():
                grads[lax.rem(s, 2), 0] = g_real
                grads[lax.rem(s, 2), 1] = g_imag

                @pl.when(step > 0)
                def _():
                    finish(s + 1)

            @pl.when(helps)
            def _():
                side[s, 0] = g_real.astype(side.dtype)
                side[s, 1] = g_imag.astype(side.dtype)
                side_out(s).start()

    @pl.when(helps)
    def _():
        @pl.loop(0, sections)
        def _(s):
            side_out(s).wait_send()

    @pl.when(works)
    def _():
        finish(0)
        term_own().wait()

    def arrived(j, k):
        return pltpu.make_async_remote_copy(
            src_ref=made.at[0, 0],
            dst_ref=terms_ref.at[j, k],
            send_sem=made_sem.at[0, 0],
            recv_sem=terms_sem.at[j, k],
            device_id=worker_of(j, k, lat, lats, stride),
            device_id_type=MESH,
        )

    def pass_on(k):
        return pltpu.make_async_remote_copy(
            src_ref=terms_ref.at[0, k],
            dst_ref=terms_ref.at[2, k],
            send_sem=pass_sem.at[k],
            recv_sem=terms_sem.at[2, k],
            device_id=ahead,
            device_id_type=MESH,
        )

    @pl.loop(0, count)
    def _(turn):
        k = count - 1 - order(turn)

        @pl.when(jnp.logical_not(mine(0, k)))
        def _():
            arrived(0, k).wait_recv()

        pass_on(k).start()

    @pl.when(works)
    def _():
        @pl.loop(0, sections)
        def _(s):
            for j in range(SENT):

                @pl.when((s != me) if j == 0 else True)
                def _():
                    term_out(s, j).wait_send()

            whole_out(s).wait_send()

    @pl.loop(0, count)
    def _(k):
        rows_out(k).wait_send()
        block_out(1, k).wait_send()
        arrived(1, k).wait_recv()
        pass_on(k).wait()

        @pl.when(jnp.logical_not(mine(0, k)))
        def _():
            block_out(0, k).wait_send()


def on_device(object_slices, probe, positions, measured):
    pixels = probe.shape[-1]
    tile_rows, cols = object_slices.shape[2:]
    count = positions.shape[0]
    sections = lax.axis_size("depth")
    lats = lax.axis_size("lat")
    low = jnp.bfloat16
    vmem = pl.BlockSpec(memory_space=pltpu.VMEM)
    smem = pl.BlockSpec(memory_space=pltpu.SMEM)
    anywhere = pl.BlockSpec(memory_space=pl.ANY)
    block = (2, tile_rows, pixels)
    tables = host_tables(pixels)
    assert probe.shape[0] % 2 == 0 and lats % 2 == 0 and (sections // count) % 2 == 0
    shared = (probe.shape[0] // 2,) + probe.shape[1:]
    patch = (2, pixels, pixels)
    near = [positions] + [shifted(positions, "lat", j) for j in range(1, TILES)]

    blocks = pl.pallas_call(
        extract_kernel,
        out_shape=jax.ShapeDtypeStruct((TILES, count) + block, low),
        in_specs=[smem] * TILES + [vmem],
        out_specs=vmem,
        compiler_params=pltpu.CompilerParams(vmem_limit_bytes=VMEM_BYTES),
        name="extract",
    )(*near, object_slices)

    terms = pl.pallas_call(
        functools.partial(main_kernel, count, sections, lats),
        out_shape=jax.ShapeDtypeStruct((TILES, count) + block, low),
        in_specs=[smem, vmem] + [anywhere] * 3,
        out_specs=anywhere,
        scratch_shapes=[
            pltpu.VMEM((count,) + block, low),
            pltpu.VMEM((count,) + block, low),
            pltpu.VMEM((sections, SENT) + block, low),
            pltpu.VMEM((sections, SENT) + block, low),
            pltpu.VMEM((sections,) + patch, low),
            pltpu.VMEM((sections,) + patch, low),
            pltpu.VMEM((2,) + patch, jnp.float32),
            pltpu.VMEM(patch, jnp.float32),
            pltpu.VMEM((sections + 1,) + shared, low),
            pltpu.VMEM(shared, low),
            pltpu.VMEM(tables.shape, low),
            pltpu.VMEM(shared, jnp.float32),
            pltpu.VMEM(measured.shape[1:], jnp.float32),
            pltpu.SemaphoreType.DMA((3,)),
            pltpu.SemaphoreType.DMA((SENT, count)),
            pltpu.SemaphoreType.DMA((sections, SENT)),
            pltpu.SemaphoreType.DMA((2,)),
            pltpu.SemaphoreType.DMA((sections, SENT)),
            pltpu.SemaphoreType.DMA((TILES, count)),
            pltpu.SemaphoreType.DMA((count,)),
            pltpu.SemaphoreType.DMA((count,)),
            pltpu.SemaphoreType.DMA((count,)),
            pltpu.SemaphoreType.DMA((sections,)),
            pltpu.SemaphoreType.DMA((sections,)),
            pltpu.SemaphoreType.DMA((sections,)),
            pltpu.SemaphoreType.DMA((sections,)),
            pltpu.SemaphoreType.DMA((2,)),
        ],
        compiler_params=pltpu.CompilerParams(
            collective_id=0, has_side_effects=True, vmem_limit_bytes=VMEM_BYTES
        ),
        name="windows",
    )(positions, blocks, probe, measured, tables)

    return pl.pallas_call(
        gather_kernel,
        out_shape=jax.ShapeDtypeStruct(object_slices.shape, jnp.float32),
        in_specs=[smem] * TILES + [vmem],
        out_specs=vmem,
        compiler_params=pltpu.CompilerParams(vmem_limit_bytes=VMEM_BYTES),
        name="gather",
    )(*near, terms)


def solution(mesh):
    return jax.shard_map(
        on_device,
        mesh=mesh,
        in_specs=(P("depth", None, "lat", None), P(), P("lat", None), P("lat", None, None)),
        out_specs=P("depth", None, "lat", None),
        check_vma=False,
    )
```

```python
import functools
import math

import jax
import jax.numpy as jnp
import ml_dtypes
import numpy as np
from jax import lax
from jax.experimental import pallas as pl
from jax.experimental.pallas import tpu as pltpu
from jax.sharding import PartitionSpec as P

fresnel = 0.5
MESH = pl.DeviceIdType.MESH
TILES = 3
SENT = 2
LANES = 128
VMEM_BYTES = 48 * 1024 * 1024


def shifted(block, axis, distance):
    devices = range(lax.axis_size(axis))
    route = [((i - distance) % len(devices), i) for i in devices]
    return lax.ppermute(block, axis, route)


def host_tables(pixels):
    idx = np.arange(pixels)
    angle = 2.0 * np.pi * (np.outer(idx, idx) % pixels) / pixels
    far = np.exp(-1j * angle) / math.sqrt(pixels)
    freq = np.where(idx < pixels // 2, idx, idx - pixels).astype(np.float64)
    prop = (np.conj(far) * np.exp(-1j * np.pi * fresnel * freq * freq / pixels)[None, :]) @ far

    def block(table):
        return np.block([[table.real, -table.imag], [table.imag, table.real]])

    prop_block, far_block = block(prop), block(far)
    tables = np.stack([prop_block, prop_block.T, far_block, far_block.T])
    high = tables.astype(ml_dtypes.bfloat16)
    rest = (tables - high.astype(np.float64)).astype(ml_dtypes.bfloat16)
    return jnp.asarray(np.stack([high, rest], axis=1))


def window_place(positions_ref, k, tile_rows, col_tiles):
    row = lax.rem(positions_ref[k, 0], tile_rows)
    col = positions_ref[k, 1]
    first = jnp.minimum(col // LANES, col_tiles - 3)
    return row, first, col - first * LANES


def upper_rows(shape, keep):
    return lax.broadcasted_iota(jnp.int32, shape, 0) < keep


def extract_kernel(near0_ref, near1_ref, near2_ref, tile_ref, blocks_ref):
    near = (near0_ref, near1_ref, near2_ref)
    _, _, tile_rows, cols = tile_ref.shape
    _, count, _, _, pixels = blocks_ref.shape
    wide = pixels + LANES

    for j in range(TILES):

        @pl.loop(0, count)
        def _(k):
            row, first, shift = window_place(near[j], k, tile_rows, cols // LANES)
            start = pl.multiple_of(first * LANES, LANES)
            piece = tile_ref[0, 0, :, pl.ds(start, wide)]
            piece = pltpu.roll(piece, lax.rem(wide - shift, wide), 1)[:, :pixels]
            piece = pltpu.roll(piece, lax.rem(tile_rows - row, tile_rows), 0)
            blocks_ref[j, k, 0] = piece.astype(blocks_ref.dtype)


def gather_kernel(near0_ref, near1_ref, near2_ref, terms_ref, grad_ref):
    near = (near0_ref, near1_ref, near2_ref)
    _, _, tile_rows, cols = grad_ref.shape
    _, count, _, _, pixels = terms_ref.shape
    wide = pixels + LANES
    grad_ref[...] = jnp.zeros_like(grad_ref)

    for j in range(TILES):

        @pl.loop(0, count)
        def _(k):
            row, first, shift = window_place(near[j], k, tile_rows, cols // LANES)
            start = pl.multiple_of(first * LANES, LANES)
            piece = terms_ref[j, k, 0].astype(jnp.float32)
            if j != 1:
                upper = upper_rows(piece.shape, tile_rows - row)
                kept = upper if j == 0 else jnp.logical_not(upper)
                piece = jnp.where(kept, piece, 0.0)
            piece = pltpu.roll(piece, row, 0)
            piece = jnp.concatenate(
                [piece, jnp.zeros((tile_rows, LANES), jnp.float32)], axis=1
            )
            piece = pltpu.roll(piece, shift, 1)
            grad_ref[0, 0, :, pl.ds(start, wide)] += piece


def spread(count, sections, lats):
    stride = sections // count
    me = lax.axis_index("depth")
    lat = lax.axis_index("lat")
    works = (lax.rem(me, stride) == lax.rem(lat, stride)) & (me // stride < count)
    return stride, me, lat, works


def worker_of(j, k, lat, lats, stride):
    owner = lax.rem(lat - j + lats, lats)
    return {"depth": k * stride + lax.rem(owner, stride), "lat": owner}


def transform(left, right, parts, pixels):
    low = jnp.bfloat16
    stacked = jnp.concatenate(
        [jnp.concatenate([p.astype(low) for p in pair], axis=0) for pair in parts], axis=1
    )
    dot = functools.partial(jnp.dot, preferred_element_type=jnp.float32)
    middle = (dot(left[0], stacked) + dot(left[1], stacked)).astype(low)
    rows = [
        jnp.concatenate(
            [
                middle[:pixels, m * pixels : (m + 1) * pixels],
                middle[pixels:, m * pixels : (m + 1) * pixels],
            ],
            axis=1,
        )
        for m in range(len(parts))
    ]
    joined = jnp.concatenate(rows, axis=0)
    ended = dot(joined, right[0]) + dot(joined, right[1])
    return [
        (
            ended[m * pixels : (m + 1) * pixels, :pixels],
            ended[m * pixels : (m + 1) * pixels, pixels:],
        )
        for m in range(len(parts))
    ]


def main_kernel(
    count,
    sections,
    lats,
    near0_ref,
    blocks,
    probe_ref,
    measured_ref,
    tables_ref,
    terms_ref,
    merged,
    halo,
    held,
    made,
    saved,
    back,
    tables,
    start_wave,
    target,
    load_sem,
    out_sem,
    in_sem,
    own_sem,
    made_sem,
    terms_sem,
    halo_out_sem,
    halo_in_sem,
    pass_sem,
):
    tile_rows, pixels = held.shape[3:]
    modes = probe_ref.shape[0]
    stride, me, lat, works = spread(count, sections, lats)
    window = lax.rem(me // stride, count)

    def source(s, j):
        return {"depth": s, "lat": lax.rem(lat + j, lats)}

    def mine(j, k):
        return works & (window == k) if j == 0 else False

    barrier = pltpu.get_barrier_semaphore()
    for j in range(SENT):

        @pl.loop(0, count)
        def _(k):
            @pl.when(jnp.logical_not(mine(j, k)))
            def _():
                pl.semaphore_signal(
                    barrier,
                    inc=1,
                    device_id=worker_of(j, k, lat, lats, stride),
                    device_id_type=MESH,
                )

    ahead = {"depth": me, "lat": lax.rem(lat + 2, lats)}
    behind = {"depth": me, "lat": lax.rem(lat - 2 + lats, lats)}
    for peer in (ahead, behind):
        pl.semaphore_signal(barrier, inc=1, device_id=peer, device_id_type=MESH)

    loads = (
        pltpu.make_async_copy(tables_ref, tables, load_sem.at[0]),
        pltpu.make_async_copy(probe_ref, start_wave, load_sem.at[1]),
        pltpu.make_async_copy(measured_ref.at[window], target, load_sem.at[2]),
    )

    @pl.when(works)
    def _():
        for j in range(SENT):

            @pl.loop(0, sections)
            def _(s):
                @pl.when((s != me) if j == 0 else True)
                def _():
                    pl.semaphore_signal(
                        barrier, inc=1, device_id=source(s, j), device_id_type=MESH
                    )

        for load in loads:
            load.start()

    busy = works.astype(jnp.int32)
    pl.semaphore_wait(barrier, SENT * count + 2 - busy + busy * (SENT * sections - 1))

    def block_out(j, k):
        return pltpu.make_async_remote_copy(
            src_ref=merged.at[k] if j == 0 else blocks.at[j, k],
            dst_ref=held.at[me, j],
            send_sem=out_sem.at[j, k],
            recv_sem=in_sem.at[me, j],
            device_id=worker_of(j, k, lat, lats, stride),
            device_id_type=MESH,
        )

    def block_own(k):
        return pltpu.make_async_copy(merged.at[k], held.at[me, 0], own_sem.at[0])

    far_first = 1 - jnp.minimum((4 * me) // sections, 1)

    def order(turn):
        return far_first * (count - 1 - turn) + (1 - far_first) * turn

    def rows_out(k):
        return pltpu.make_async_remote_copy(
            src_ref=blocks.at[2, k],
            dst_ref=halo.at[k],
            send_sem=halo_out_sem.at[k],
            recv_sem=halo_in_sem.at[k],
            device_id=behind,
            device_id_type=MESH,
        )

    @pl.loop(0, count)
    def _(turn):
        rows_out(order(turn)).start()

    @pl.loop(0, count)
    def _(turn):
        block_out(1, order(turn)).start()

    def upper(k):
        keep = tile_rows - lax.rem(near0_ref[k, 0], tile_rows)
        return upper_rows((tile_rows, pixels), keep)

    @pl.loop(0, count)
    def _(turn):
        k = order(turn)
        rows_out(k).wait_recv()
        for part in range(2):
            merged[k, part] = jnp.where(
                upper(k),
                blocks[0, k, part].astype(jnp.float32),
                halo[k, part].astype(jnp.float32),
            ).astype(merged.dtype)
        own = mine(0, k)

        @pl.when(own)
        def _():
            block_own(k).start()

        @pl.when(jnp.logical_not(own))
        def _():
            block_out(0, k).start()

    def term_out(s, j):
        return pltpu.make_async_remote_copy(
            src_ref=made.at[s, j],
            dst_ref=terms_ref.at[j, window],
            send_sem=made_sem.at[s, j],
            recv_sem=terms_sem.at[j, window],
            device_id=source(s, j),
            device_id_type=MESH,
        )

    def term_own():
        return pltpu.make_async_copy(
            made.at[me, 0], terms_ref.at[0, window], own_sem.at[1]
        )

    def patch(s):
        mask = upper(window)
        out = []
        for part in range(2):
            a, b = (held[s, j, part].astype(jnp.float32) for j in range(SENT))
            out.append(
                jnp.concatenate([jnp.where(mask, a, b), jnp.where(mask, b, a)], axis=0)
            )
        return out

    @pl.when(works)
    def _():
        for load in loads:
            load.wait()
        saved[0] = start_wave[...].astype(jnp.bfloat16)
        block_own(window).wait()

        @pl.loop(0, sections)
        def _(s):
            for j in range(SENT):

                @pl.when((s != me) if j == 0 else True)
                def _():
                    pltpu.make_async_remote_copy(
                        src_ref=blocks.at[0, 0],
                        dst_ref=held.at[s, j],
                        send_sem=out_sem.at[0, 0],
                        recv_sem=in_sem.at[s, j],
                        device_id=source(s, j),
                        device_id_type=MESH,
                    ).wait_recv()

            p_real, p_imag = patch(s)
            lit = []
            for m in range(modes):
                w_real = saved[s, m, 0].astype(jnp.float32)
                w_imag = saved[s, m, 1].astype(jnp.float32)
                lit.append(
                    (p_real * w_real - p_imag * w_imag, p_real * w_imag + p_imag * w_real)
                )
            moved = transform(tables.at[0], tables.at[1], lit, pixels)
            for m in range(modes):
                for part in range(2):
                    saved[s + 1, m, part] = moved[m][part].astype(jnp.bfloat16)

        last = [(saved[sections, m, 0], saved[sections, m, 1]) for m in range(modes)]
        far = transform(tables.at[2], tables.at[3], last, pixels)
        resid = -target[...]
        for real, imag in far:
            resid = resid + (real * real + imag * imag)
        seed = [(resid * real, resid * imag) for real, imag in far]
        seed = transform(tables.at[3], tables.at[2], seed, pixels)
        for m in range(modes):
            for part in range(2):
                back[m, part] = seed[m][part].astype(jnp.bfloat16)

        @pl.loop(0, sections)
        def _(step):
            s = sections - 1 - step
            p_real, p_imag = patch(s)
            waves = [(back[m, 0], back[m, 1]) for m in range(modes)]
            lit = transform(tables.at[1], tables.at[0], waves, pixels)
            g_real = jnp.zeros((pixels, pixels), jnp.float32)
            g_imag = jnp.zeros((pixels, pixels), jnp.float32)
            for m in range(modes):
                l_real, l_imag = lit[m]
                w_real = saved[s, m, 0].astype(jnp.float32)
                w_imag = saved[s, m, 1].astype(jnp.float32)
                g_real = g_real + (w_real * l_real + w_imag * l_imag)
                g_imag = g_imag + (w_real * l_imag - w_imag * l_real)
                back[m, 0] = (p_real * l_real + p_imag * l_imag).astype(jnp.bfloat16)
                back[m, 1] = (p_real * l_imag - p_imag * l_real).astype(jnp.bfloat16)
            mask = upper(window)
            for part, term in enumerate((g_real, g_imag)):
                top, bottom = term[:tile_rows], term[tile_rows:]
                made[s, 0, part] = jnp.where(mask, top, bottom).astype(made.dtype)
                made[s, 1, part] = jnp.where(mask, bottom, top).astype(made.dtype)
            for j in range(SENT):

                @pl.when((s != me) if j == 0 else True)
                def _():
                    term_out(s, j).start()

            @pl.when(s == me)
            def _():
                term_own().start()

        term_own().wait()

    def arrived(j, k):
        return pltpu.make_async_remote_copy(
            src_ref=made.at[0, 0],
            dst_ref=terms_ref.at[j, k],
            send_sem=made_sem.at[0, 0],
            recv_sem=terms_sem.at[j, k],
            device_id=worker_of(j, k, lat, lats, stride),
            device_id_type=MESH,
        )

    def pass_on(k):
        return pltpu.make_async_remote_copy(
            src_ref=terms_ref.at[0, k],
            dst_ref=terms_ref.at[2, k],
            send_sem=pass_sem.at[k],
            recv_sem=terms_sem.at[2, k],
            device_id=ahead,
            device_id_type=MESH,
        )

    upper_half = (2 * me) // sections

    def back_order(turn):
        return upper_half * (count - 1 - turn) + (1 - upper_half) * turn

    @pl.loop(0, count)
    def _(turn):
        k = back_order(turn)

        @pl.when(jnp.logical_not(mine(0, k)))
        def _():
            arrived(0, k).wait_recv()

        pass_on(k).start()

    @pl.when(works)
    def _():
        @pl.loop(0, sections)
        def _(s):
            for j in range(SENT):

                @pl.when((s != me) if j == 0 else True)
                def _():
                    term_out(s, j).wait_send()

    @pl.loop(0, count)
    def _(k):
        rows_out(k).wait_send()
        block_out(1, k).wait_send()
        arrived(1, k).wait_recv()
        pass_on(k).wait()

        @pl.when(jnp.logical_not(mine(0, k)))
        def _():
            block_out(0, k).wait_send()


def on_device(object_slices, probe, positions, measured):
    pixels = probe.shape[-1]
    tile_rows, cols = object_slices.shape[2:]
    count = positions.shape[0]
    sections = lax.axis_size("depth")
    lats = lax.axis_size("lat")
    low = jnp.bfloat16
    vmem = pl.BlockSpec(memory_space=pltpu.VMEM)
    smem = pl.BlockSpec(memory_space=pltpu.SMEM)
    anywhere = pl.BlockSpec(memory_space=pl.ANY)
    block = (2, tile_rows, pixels)
    tile_part = pl.BlockSpec((1, 1, tile_rows, cols), lambda part: (0, part, 0, 0))
    blocks_part = pl.BlockSpec(
        (TILES, count, 1, tile_rows, pixels), lambda part: (0, 0, part, 0, 0)
    )
    tables = host_tables(pixels)
    near = [positions] + [shifted(positions, "lat", j) for j in range(1, TILES)]

    blocks = pl.pallas_call(
        extract_kernel,
        out_shape=jax.ShapeDtypeStruct((TILES, count) + block, low),
        grid=(2,),
        in_specs=[smem] * TILES + [tile_part],
        out_specs=blocks_part,
        compiler_params=pltpu.CompilerParams(vmem_limit_bytes=VMEM_BYTES),
        name="extract",
    )(*near, object_slices)

    terms = pl.pallas_call(
        functools.partial(main_kernel, count, sections, lats),
        out_shape=jax.ShapeDtypeStruct((TILES, count) + block, low),
        in_specs=[smem, vmem] + [anywhere] * 3,
        out_specs=anywhere,
        scratch_shapes=[
            pltpu.VMEM((count,) + block, low),
            pltpu.VMEM((count,) + block, low),
            pltpu.VMEM((sections, SENT) + block, low),
            pltpu.VMEM((sections, SENT) + block, low),
            pltpu.VMEM((sections + 1,) + probe.shape, low),
            pltpu.VMEM(probe.shape, low),
            pltpu.VMEM(tables.shape, low),
            pltpu.VMEM(probe.shape, jnp.float32),
            pltpu.VMEM(measured.shape[1:], jnp.float32),
            pltpu.SemaphoreType.DMA((3,)),
            pltpu.SemaphoreType.DMA((SENT, count)),
            pltpu.SemaphoreType.DMA((sections, SENT)),
            pltpu.SemaphoreType.DMA((2,)),
            pltpu.SemaphoreType.DMA((sections, SENT)),
            pltpu.SemaphoreType.DMA((TILES, count)),
            pltpu.SemaphoreType.DMA((count,)),
            pltpu.SemaphoreType.DMA((count,)),
            pltpu.SemaphoreType.DMA((count,)),
        ],
        compiler_params=pltpu.CompilerParams(
            collective_id=0, has_side_effects=True, vmem_limit_bytes=VMEM_BYTES
        ),
        name="windows",
    )(positions, blocks, probe, measured, tables)

    return pl.pallas_call(
        gather_kernel,
        out_shape=jax.ShapeDtypeStruct(object_slices.shape, jnp.float32),
        grid=(2,),
        in_specs=[smem] * TILES + [blocks_part],
        out_specs=tile_part,
        compiler_params=pltpu.CompilerParams(vmem_limit_bytes=VMEM_BYTES),
        name="gather",
    )(*near, terms)


def solution(mesh):
    return jax.shard_map(
        on_device,
        mesh=mesh,
        in_specs=(P("depth", None, "lat", None), P(), P("lat", None), P("lat", None, None)),
        out_specs=P("depth", None, "lat", None),
        check_vma=False,
    )
```

```python
import functools
import math

import jax
import jax.numpy as jnp
import ml_dtypes
import numpy as np
from jax import lax
from jax.experimental import pallas as pl
from jax.experimental.pallas import tpu as pltpu
from jax.sharding import PartitionSpec as P

fresnel = 0.5
MESH = pl.DeviceIdType.MESH
TILES = 3
SENT = 2
LANES = 128
VMEM_BYTES = 48 * 1024 * 1024


def shifted(block, axis, distance):
    devices = range(lax.axis_size(axis))
    route = [((i - distance) % len(devices), i) for i in devices]
    return lax.ppermute(block, axis, route)


def host_tables(pixels):
    idx = np.arange(pixels)
    angle = 2.0 * np.pi * (np.outer(idx, idx) % pixels) / pixels
    far = np.exp(-1j * angle) / math.sqrt(pixels)
    freq = np.where(idx < pixels // 2, idx, idx - pixels).astype(np.float64)
    prop = (np.conj(far) * np.exp(-1j * np.pi * fresnel * freq * freq / pixels)[None, :]) @ far

    def block(table):
        return np.block([[table.real, -table.imag], [table.imag, table.real]])

    prop_block, far_block = block(prop), block(far)
    tables = np.stack([prop_block, prop_block.T, far_block, far_block.T])
    high = tables.astype(ml_dtypes.bfloat16)
    rest = (tables - high.astype(np.float64)).astype(ml_dtypes.bfloat16)
    return jnp.asarray(np.stack([high, rest], axis=1))


def window_place(positions_ref, k, tile_rows, col_tiles):
    row = lax.rem(positions_ref[k, 0], tile_rows)
    col = positions_ref[k, 1]
    first = jnp.minimum(col // LANES, col_tiles - 3)
    return row, first, col - first * LANES


def upper_rows(shape, keep):
    return lax.broadcasted_iota(jnp.int32, shape, 0) < keep


def extract_kernel(near0_ref, near1_ref, near2_ref, tile_ref, blocks_ref):
    near = (near0_ref, near1_ref, near2_ref)
    _, _, tile_rows, cols = tile_ref.shape
    _, count, _, _, pixels = blocks_ref.shape
    wide = pixels + LANES

    for j in range(TILES):

        @pl.loop(0, count)
        def _(k):
            row, first, shift = window_place(near[j], k, tile_rows, cols // LANES)
            start = pl.multiple_of(first * LANES, LANES)
            for part in range(2):
                piece = tile_ref[0, part, :, pl.ds(start, wide)]
                piece = pltpu.roll(piece, lax.rem(wide - shift, wide), 1)[:, :pixels]
                piece = pltpu.roll(piece, lax.rem(tile_rows - row, tile_rows), 0)
                blocks_ref[j, k, part] = piece.astype(blocks_ref.dtype)


def gather_kernel(near0_ref, near1_ref, near2_ref, terms_ref, grad_ref):
    near = (near0_ref, near1_ref, near2_ref)
    _, _, tile_rows, cols = grad_ref.shape
    _, count, _, _, pixels = terms_ref.shape
    wide = pixels + LANES
    grad_ref[...] = jnp.zeros_like(grad_ref)

    for j in range(TILES):

        @pl.loop(0, count)
        def _(k):
            row, first, shift = window_place(near[j], k, tile_rows, cols // LANES)
            start = pl.multiple_of(first * LANES, LANES)
            for part in range(2):
                piece = terms_ref[j, k, part].astype(jnp.float32)
                if j != 1:
                    upper = upper_rows(piece.shape, tile_rows - row)
                    kept = upper if j == 0 else jnp.logical_not(upper)
                    piece = jnp.where(kept, piece, 0.0)
                piece = pltpu.roll(piece, row, 0)
                piece = jnp.concatenate(
                    [piece, jnp.zeros((tile_rows, LANES), jnp.float32)], axis=1
                )
                piece = pltpu.roll(piece, shift, 1)
                grad_ref[0, part, :, pl.ds(start, wide)] += piece


def spread(count, sections, lats):
    stride = sections // count
    me = lax.axis_index("depth")
    lat = lax.axis_index("lat")
    works = (lax.rem(me, stride) == lax.rem(lat, stride)) & (me // stride < count)
    return stride, me, lat, works


def worker_of(j, k, lat, lats, stride):
    owner = lax.rem(lat - j + lats, lats)
    return {"depth": k * stride + lax.rem(owner, stride), "lat": owner}


def transform(left, right, parts, pixels):
    low = jnp.bfloat16
    stacked = jnp.concatenate(
        [jnp.concatenate([p.astype(low) for p in pair], axis=0) for pair in parts], axis=1
    )
    dot = functools.partial(jnp.dot, preferred_element_type=jnp.float32)
    middle = (dot(left[0], stacked) + dot(left[1], stacked)).astype(low)
    rows = [
        jnp.concatenate(
            [
                middle[:pixels, m * pixels : (m + 1) * pixels],
                middle[pixels:, m * pixels : (m + 1) * pixels],
            ],
            axis=1,
        )
        for m in range(len(parts))
    ]
    joined = jnp.concatenate(rows, axis=0)
    ended = dot(joined, right[0]) + dot(joined, right[1])
    return [
        (
            ended[m * pixels : (m + 1) * pixels, :pixels],
            ended[m * pixels : (m + 1) * pixels, pixels:],
        )
        for m in range(len(parts))
    ]


def main_kernel(
    count,
    sections,
    lats,
    near0_ref,
    blocks,
    probe_ref,
    measured_ref,
    tables_ref,
    terms_ref,
    merged,
    halo,
    held,
    made,
    saved,
    back,
    tables,
    start_wave,
    target,
    load_sem,
    out_sem,
    in_sem,
    own_sem,
    made_sem,
    terms_sem,
    halo_out_sem,
    halo_in_sem,
    pass_sem,
):
    tile_rows, pixels = held.shape[3:]
    modes = probe_ref.shape[0]
    stride, me, lat, works = spread(count, sections, lats)
    window = lax.rem(me // stride, count)

    def source(s, j):
        return {"depth": s, "lat": lax.rem(lat + j, lats)}

    def mine(j, k):
        return works & (window == k) if j == 0 else False

    barrier = pltpu.get_barrier_semaphore()
    for j in range(SENT):

        @pl.loop(0, count)
        def _(k):
            @pl.when(jnp.logical_not(mine(j, k)))
            def _():
                pl.semaphore_signal(
                    barrier,
                    inc=1,
                    device_id=worker_of(j, k, lat, lats, stride),
                    device_id_type=MESH,
                )

    ahead = {"depth": me, "lat": lax.rem(lat + 2, lats)}
    behind = {"depth": me, "lat": lax.rem(lat - 2 + lats, lats)}
    for peer in (ahead, behind):
        pl.semaphore_signal(barrier, inc=1, device_id=peer, device_id_type=MESH)

    loads = (
        pltpu.make_async_copy(tables_ref, tables, load_sem.at[0]),
        pltpu.make_async_copy(probe_ref, start_wave, load_sem.at[1]),
        pltpu.make_async_copy(measured_ref.at[window], target, load_sem.at[2]),
    )

    @pl.when(works)
    def _():
        for j in range(SENT):

            @pl.loop(0, sections)
            def _(s):
                @pl.when((s != me) if j == 0 else True)
                def _():
                    pl.semaphore_signal(
                        barrier, inc=1, device_id=source(s, j), device_id_type=MESH
                    )

        for load in loads:
            load.start()

    busy = works.astype(jnp.int32)
    pl.semaphore_wait(barrier, SENT * count + 2 - busy + busy * (SENT * sections - 1))

    def block_out(j, k):
        return pltpu.make_async_remote_copy(
            src_ref=merged.at[k] if j == 0 else blocks.at[j, k],
            dst_ref=held.at[me, j],
            send_sem=out_sem.at[j, k],
            recv_sem=in_sem.at[me, j],
            device_id=worker_of(j, k, lat, lats, stride),
            device_id_type=MESH,
        )

    def block_own(k):
        return pltpu.make_async_copy(merged.at[k], held.at[me, 0], own_sem.at[0])

    far_first = 1 - jnp.minimum((4 * me) // sections, 1)

    def order(turn):
        return far_first * (count - 1 - turn) + (1 - far_first) * turn

    def rows_out(k):
        return pltpu.make_async_remote_copy(
            src_ref=blocks.at[2, k],
            dst_ref=halo.at[k],
            send_sem=halo_out_sem.at[k],
            recv_sem=halo_in_sem.at[k],
            device_id=behind,
            device_id_type=MESH,
        )

    @pl.loop(0, count)
    def _(turn):
        rows_out(order(turn)).start()

    @pl.loop(0, count)
    def _(turn):
        block_out(1, order(turn)).start()

    def upper(k):
        keep = tile_rows - lax.rem(near0_ref[k, 0], tile_rows)
        return upper_rows((tile_rows, pixels), keep)

    @pl.loop(0, count)
    def _(turn):
        k = order(turn)
        rows_out(k).wait_recv()
        for part in range(2):
            merged[k, part] = jnp.where(
                upper(k),
                blocks[0, k, part].astype(jnp.float32),
                halo[k, part].astype(jnp.float32),
            ).astype(merged.dtype)
        own = mine(0, k)

        @pl.when(own)
        def _():
            block_own(k).start()

        @pl.when(jnp.logical_not(own))
        def _():
            block_out(0, k).start()

    def term_out(s, j):
        return pltpu.make_async_remote_copy(
            src_ref=made.at[s, j],
            dst_ref=terms_ref.at[j, window],
            send_sem=made_sem.at[s, j],
            recv_sem=terms_sem.at[j, window],
            device_id=source(s, j),
            device_id_type=MESH,
        )

    def term_own():
        return pltpu.make_async_copy(
            made.at[me, 0], terms_ref.at[0, window], own_sem.at[1]
        )

    def patch(s):
        mask = upper(window)
        out = []
        for part in range(2):
            a, b = (held[s, j, part].astype(jnp.float32) for j in range(SENT))
            out.append(
                jnp.concatenate([jnp.where(mask, a, b), jnp.where(mask, b, a)], axis=0)
            )
        return out

    @pl.when(works)
    def _():
        for load in loads:
            load.wait()
        saved[0] = start_wave[...].astype(jnp.bfloat16)
        block_own(window).wait()

        @pl.loop(0, sections)
        def _(s):
            for j in range(SENT):

                @pl.when((s != me) if j == 0 else True)
                def _():
                    pltpu.make_async_remote_copy(
                        src_ref=blocks.at[0, 0],
                        dst_ref=held.at[s, j],
                        send_sem=out_sem.at[0, 0],
                        recv_sem=in_sem.at[s, j],
                        device_id=source(s, j),
                        device_id_type=MESH,
                    ).wait_recv()

            p_real, p_imag = patch(s)
            lit = []
            for m in range(modes):
                w_real = saved[s, m, 0].astype(jnp.float32)
                w_imag = saved[s, m, 1].astype(jnp.float32)
                lit.append(
                    (p_real * w_real - p_imag * w_imag, p_real * w_imag + p_imag * w_real)
                )
            moved = transform(tables.at[0], tables.at[1], lit, pixels)
            for m in range(modes):
                for part in range(2):
                    saved[s + 1, m, part] = moved[m][part].astype(jnp.bfloat16)

        last = [(saved[sections, m, 0], saved[sections, m, 1]) for m in range(modes)]
        far = transform(tables.at[2], tables.at[3], last, pixels)
        resid = -target[...]
        for real, imag in far:
            resid = resid + (real * real + imag * imag)
        seed = [(resid * real, resid * imag) for real, imag in far]
        seed = transform(tables.at[3], tables.at[2], seed, pixels)
        for m in range(modes):
            for part in range(2):
                back[m, part] = seed[m][part].astype(jnp.bfloat16)

        @pl.loop(0, sections)
        def _(step):
            s = sections - 1 - step
            p_real, p_imag = patch(s)
            waves = [(back[m, 0], back[m, 1]) for m in range(modes)]
            lit = transform(tables.at[1], tables.at[0], waves, pixels)
            g_real = jnp.zeros((pixels, pixels), jnp.float32)
            g_imag = jnp.zeros((pixels, pixels), jnp.float32)
            for m in range(modes):
                l_real, l_imag = lit[m]
                w_real = saved[s, m, 0].astype(jnp.float32)
                w_imag = saved[s, m, 1].astype(jnp.float32)
                g_real = g_real + (w_real * l_real + w_imag * l_imag)
                g_imag = g_imag + (w_real * l_imag - w_imag * l_real)
                back[m, 0] = (p_real * l_real + p_imag * l_imag).astype(jnp.bfloat16)
                back[m, 1] = (p_real * l_imag - p_imag * l_real).astype(jnp.bfloat16)
            mask = upper(window)
            for part, term in enumerate((g_real, g_imag)):
                top, bottom = term[:tile_rows], term[tile_rows:]
                made[s, 0, part] = jnp.where(mask, top, bottom).astype(made.dtype)
                made[s, 1, part] = jnp.where(mask, bottom, top).astype(made.dtype)
            for j in range(SENT):

                @pl.when((s != me) if j == 0 else True)
                def _():
                    term_out(s, j).start()

            @pl.when(s == me)
            def _():
                term_own().start()

        term_own().wait()

    def arrived(j, k):
        return pltpu.make_async_remote_copy(
            src_ref=made.at[0, 0],
            dst_ref=terms_ref.at[j, k],
            send_sem=made_sem.at[0, 0],
            recv_sem=terms_sem.at[j, k],
            device_id=worker_of(j, k, lat, lats, stride),
            device_id_type=MESH,
        )

    def pass_on(k):
        return pltpu.make_async_remote_copy(
            src_ref=terms_ref.at[0, k],
            dst_ref=terms_ref.at[2, k],
            send_sem=pass_sem.at[k],
            recv_sem=terms_sem.at[2, k],
            device_id=ahead,
            device_id_type=MESH,
        )

    upper_half = (2 * me) // sections

    def back_order(turn):
        return upper_half * (count - 1 - turn) + (1 - upper_half) * turn

    @pl.loop(0, count)
    def _(turn):
        k = back_order(turn)

        @pl.when(jnp.logical_not(mine(0, k)))
        def _():
            arrived(0, k).wait_recv()

        pass_on(k).start()

    @pl.when(works)
    def _():
        @pl.loop(0, sections)
        def _(s):
            for j in range(SENT):

                @pl.when((s != me) if j == 0 else True)
                def _():
                    term_out(s, j).wait_send()

    @pl.loop(0, count)
    def _(k):
        rows_out(k).wait_send()
        block_out(1, k).wait_send()
        arrived(1, k).wait_recv()
        pass_on(k).wait()

        @pl.when(jnp.logical_not(mine(0, k)))
        def _():
            block_out(0, k).wait_send()


def on_device(object_slices, probe, positions, measured):
    pixels = probe.shape[-1]
    tile_rows, cols = object_slices.shape[2:]
    count = positions.shape[0]
    sections = lax.axis_size("depth")
    lats = lax.axis_size("lat")
    low = jnp.bfloat16
    vmem = pl.BlockSpec(memory_space=pltpu.VMEM)
    smem = pl.BlockSpec(memory_space=pltpu.SMEM)
    anywhere = pl.BlockSpec(memory_space=pl.ANY)
    block = (2, tile_rows, pixels)
    tables = host_tables(pixels)
    near = [positions] + [shifted(positions, "lat", j) for j in range(1, TILES)]

    blocks = pl.pallas_call(
        extract_kernel,
        out_shape=jax.ShapeDtypeStruct((TILES, count) + block, low),
        in_specs=[smem] * TILES + [vmem],
        out_specs=vmem,
        compiler_params=pltpu.CompilerParams(vmem_limit_bytes=VMEM_BYTES),
        name="extract",
    )(*near, object_slices)

    terms = pl.pallas_call(
        functools.partial(main_kernel, count, sections, lats),
        out_shape=jax.ShapeDtypeStruct((TILES, count) + block, low),
        in_specs=[smem, vmem] + [anywhere] * 3,
        out_specs=anywhere,
        scratch_shapes=[
            pltpu.VMEM((count,) + block, low),
            pltpu.VMEM((count,) + block, low),
            pltpu.VMEM((sections, SENT) + block, low),
            pltpu.VMEM((sections, SENT) + block, low),
            pltpu.VMEM((sections + 1,) + probe.shape, low),
            pltpu.VMEM(probe.shape, low),
            pltpu.VMEM(tables.shape, low),
            pltpu.VMEM(probe.shape, jnp.float32),
            pltpu.VMEM(measured.shape[1:], jnp.float32),
            pltpu.SemaphoreType.DMA((3,)),
            pltpu.SemaphoreType.DMA((SENT, count)),
            pltpu.SemaphoreType.DMA((sections, SENT)),
            pltpu.SemaphoreType.DMA((2,)),
            pltpu.SemaphoreType.DMA((sections, SENT)),
            pltpu.SemaphoreType.DMA((TILES, count)),
            pltpu.SemaphoreType.DMA((count,)),
            pltpu.SemaphoreType.DMA((count,)),
            pltpu.SemaphoreType.DMA((count,)),
        ],
        compiler_params=pltpu.CompilerParams(
            collective_id=0, has_side_effects=True, vmem_limit_bytes=VMEM_BYTES
        ),
        name="windows",
    )(positions, blocks, probe, measured, tables)

    return pl.pallas_call(
        gather_kernel,
        out_shape=jax.ShapeDtypeStruct(object_slices.shape, jnp.float32),
        in_specs=[smem] * TILES + [vmem],
        out_specs=vmem,
        compiler_params=pltpu.CompilerParams(vmem_limit_bytes=VMEM_BYTES),
        name="gather",
    )(*near, terms)


def solution(mesh):
    return jax.shard_map(
        on_device,
        mesh=mesh,
        in_specs=(P("depth", None, "lat", None), P(), P("lat", None), P("lat", None, None)),
        out_specs=P("depth", None, "lat", None),
        check_vma=False,
    )
```

```python
import functools
import math

import jax
import jax.numpy as jnp
import ml_dtypes
import numpy as np
from jax import lax
from jax.experimental import pallas as pl
from jax.experimental.pallas import tpu as pltpu
from jax.sharding import PartitionSpec as P

fresnel = 0.5
MESH = pl.DeviceIdType.MESH
TILES = 3
SENT = 2
LANES = 128
VMEM_BYTES = 48 * 1024 * 1024


def shifted(block, axis, distance):
    devices = range(lax.axis_size(axis))
    route = [((i - distance) % len(devices), i) for i in devices]
    return lax.ppermute(block, axis, route)


def host_tables(pixels):
    idx = np.arange(pixels)
    angle = 2.0 * np.pi * (np.outer(idx, idx) % pixels) / pixels
    far = np.exp(-1j * angle) / math.sqrt(pixels)
    freq = np.where(idx < pixels // 2, idx, idx - pixels).astype(np.float64)
    prop = (np.conj(far) * np.exp(-1j * np.pi * fresnel * freq * freq / pixels)[None, :]) @ far

    def block(table):
        return np.block([[table.real, -table.imag], [table.imag, table.real]])

    prop_block, far_block = block(prop), block(far)
    tables = np.stack([prop_block, prop_block.T, far_block, far_block.T])
    high = tables.astype(ml_dtypes.bfloat16)
    rest = (tables - high.astype(np.float64)).astype(ml_dtypes.bfloat16)
    return jnp.asarray(np.stack([high, rest], axis=1))


def window_place(positions_ref, k, tile_rows, col_tiles):
    row = lax.rem(positions_ref[k, 0], tile_rows)
    col = positions_ref[k, 1]
    first = jnp.minimum(col // LANES, col_tiles - 3)
    return row, first, col - first * LANES


def upper_rows(shape, keep):
    return lax.broadcasted_iota(jnp.int32, shape, 0) < keep


def extract_kernel(*refs):
    *near, tile_ref, blocks_ref = refs
    _, _, tile_rows, cols = tile_ref.shape
    _, count, _, _, pixels = blocks_ref.shape
    wide = pixels + LANES

    for j in range(len(near)):

        @pl.loop(0, count)
        def _(k):
            row, first, shift = window_place(near[j], k, tile_rows, cols // LANES)
            start = pl.multiple_of(first * LANES, LANES)
            for part in range(2):
                piece = tile_ref[0, part, :, pl.ds(start, wide)]
                piece = pltpu.roll(piece, lax.rem(wide - shift, wide), 1)[:, :pixels]
                piece = pltpu.roll(piece, lax.rem(tile_rows - row, tile_rows), 0)
                blocks_ref[j, k, part] = piece.astype(blocks_ref.dtype)


def gather_kernel(near0_ref, near1_ref, near2_ref, terms_ref, grad_ref):
    near = (near0_ref, near1_ref, near2_ref)
    _, _, tile_rows, cols = grad_ref.shape
    _, count, _, _, pixels = terms_ref.shape
    wide = pixels + LANES
    grad_ref[...] = jnp.zeros_like(grad_ref)

    for j in range(TILES):

        @pl.loop(0, count)
        def _(k):
            row, first, shift = window_place(near[j], k, tile_rows, cols // LANES)
            start = pl.multiple_of(first * LANES, LANES)
            for part in range(2):
                piece = terms_ref[j, k, part].astype(jnp.float32)
                if j != 1:
                    upper = upper_rows(piece.shape, tile_rows - row)
                    kept = upper if j == 0 else jnp.logical_not(upper)
                    piece = jnp.where(kept, piece, 0.0)
                piece = pltpu.roll(piece, row, 0)
                piece = jnp.concatenate(
                    [piece, jnp.zeros((tile_rows, LANES), jnp.float32)], axis=1
                )
                piece = pltpu.roll(piece, shift, 1)
                grad_ref[0, part, :, pl.ds(start, wide)] += piece


def spread(count, sections, lats):
    stride = sections // count
    me = lax.axis_index("depth")
    lat = lax.axis_index("lat")
    works = (lax.rem(me, stride) == lax.rem(lat, stride)) & (me // stride < count)
    return stride, me, lat, works


def worker_of(j, k, lat, lats, stride):
    owner = lax.rem(lat - j + lats, lats)
    return {"depth": k * stride + lax.rem(owner, stride), "lat": owner}


def transform(left, right, parts, pixels):
    low = jnp.bfloat16
    stacked = jnp.concatenate(
        [jnp.concatenate([p.astype(low) for p in pair], axis=0) for pair in parts], axis=1
    )
    dot = functools.partial(jnp.dot, preferred_element_type=jnp.float32)
    middle = (dot(left[0], stacked) + dot(left[1], stacked)).astype(low)
    rows = [
        jnp.concatenate(
            [
                middle[:pixels, m * pixels : (m + 1) * pixels],
                middle[pixels:, m * pixels : (m + 1) * pixels],
            ],
            axis=1,
        )
        for m in range(len(parts))
    ]
    joined = jnp.concatenate(rows, axis=0)
    ended = dot(joined, right[0]) + dot(joined, right[1])
    return [
        (
            ended[m * pixels : (m + 1) * pixels, :pixels],
            ended[m * pixels : (m + 1) * pixels, pixels:],
        )
        for m in range(len(parts))
    ]


def main_kernel(
    count,
    sections,
    lats,
    near0_ref,
    own_blocks,
    blocks,
    probe_ref,
    measured_ref,
    tables_ref,
    terms_ref,
    merged,
    halo,
    held,
    made,
    saved,
    back,
    tables,
    start_wave,
    target,
    load_sem,
    out_sem,
    in_sem,
    own_sem,
    made_sem,
    terms_sem,
    halo_out_sem,
    halo_in_sem,
    pass_sem,
):
    tile_rows, pixels = held.shape[3:]
    modes = probe_ref.shape[0]
    stride, me, lat, works = spread(count, sections, lats)
    window = lax.rem(me // stride, count)

    def source(s, j):
        return {"depth": s, "lat": lax.rem(lat + j, lats)}

    def mine(j, k):
        return works & (window == k) if j == 0 else False

    barrier = pltpu.get_barrier_semaphore()
    for j in range(SENT):

        @pl.loop(0, count)
        def _(k):
            @pl.when(jnp.logical_not(mine(j, k)))
            def _():
                pl.semaphore_signal(
                    barrier,
                    inc=1,
                    device_id=worker_of(j, k, lat, lats, stride),
                    device_id_type=MESH,
                )

    ahead = {"depth": me, "lat": lax.rem(lat + 2, lats)}
    behind = {"depth": me, "lat": lax.rem(lat - 2 + lats, lats)}
    for peer in (ahead, behind):
        pl.semaphore_signal(barrier, inc=1, device_id=peer, device_id_type=MESH)

    loads = (
        pltpu.make_async_copy(tables_ref, tables, load_sem.at[0]),
        pltpu.make_async_copy(probe_ref, start_wave, load_sem.at[1]),
        pltpu.make_async_copy(measured_ref.at[window], target, load_sem.at[2]),
    )

    @pl.when(works)
    def _():
        for j in range(SENT):

            @pl.loop(0, sections)
            def _(s):
                @pl.when((s != me) if j == 0 else True)
                def _():
                    pl.semaphore_signal(
                        barrier, inc=1, device_id=source(s, j), device_id_type=MESH
                    )

        for load in loads:
            load.start()

    busy = works.astype(jnp.int32)
    pl.semaphore_wait(barrier, SENT * count + 2 - busy + busy * (SENT * sections - 1))

    def block_out(j, k):
        return pltpu.make_async_remote_copy(
            src_ref=merged.at[k] if j == 0 else blocks.at[j - 1, k],
            dst_ref=held.at[me, j],
            send_sem=out_sem.at[j, k],
            recv_sem=in_sem.at[me, j],
            device_id=worker_of(j, k, lat, lats, stride),
            device_id_type=MESH,
        )

    def block_own(k):
        return pltpu.make_async_copy(merged.at[k], held.at[me, 0], own_sem.at[0])

    far_first = 1 - jnp.minimum((4 * me) // sections, 1)

    def order(turn):
        return far_first * (count - 1 - turn) + (1 - far_first) * turn

    def rows_out(k):
        return pltpu.make_async_remote_copy(
            src_ref=blocks.at[1, k],
            dst_ref=halo.at[k],
            send_sem=halo_out_sem.at[k],
            recv_sem=halo_in_sem.at[k],
            device_id=behind,
            device_id_type=MESH,
        )

    @pl.loop(0, count)
    def _(turn):
        rows_out(order(turn)).start()

    @pl.loop(0, count)
    def _(turn):
        block_out(1, order(turn)).start()

    def upper(k):
        keep = tile_rows - lax.rem(near0_ref[k, 0], tile_rows)
        return upper_rows((tile_rows, pixels), keep)

    @pl.loop(0, count)
    def _(turn):
        k = order(turn)
        rows_out(k).wait_recv()
        for part in range(2):
            merged[k, part] = jnp.where(
                upper(k),
                own_blocks[0, k, part].astype(jnp.float32),
                halo[k, part].astype(jnp.float32),
            ).astype(merged.dtype)
        own = mine(0, k)

        @pl.when(own)
        def _():
            block_own(k).start()

        @pl.when(jnp.logical_not(own))
        def _():
            block_out(0, k).start()

    def term_out(s, j):
        return pltpu.make_async_remote_copy(
            src_ref=made.at[s, j],
            dst_ref=terms_ref.at[j, window],
            send_sem=made_sem.at[s, j],
            recv_sem=terms_sem.at[j, window],
            device_id=source(s, j),
            device_id_type=MESH,
        )

    def term_own():
        return pltpu.make_async_copy(
            made.at[me, 0], terms_ref.at[0, window], own_sem.at[1]
        )

    def patch(s):
        mask = upper(window)
        out = []
        for part in range(2):
            a, b = (held[s, j, part].astype(jnp.float32) for j in range(SENT))
            out.append(
                jnp.concatenate([jnp.where(mask, a, b), jnp.where(mask, b, a)], axis=0)
            )
        return out

    @pl.when(works)
    def _():
        for load in loads:
            load.wait()
        saved[0] = start_wave[...].astype(jnp.bfloat16)
        block_own(window).wait()

        @pl.loop(0, sections)
        def _(s):
            for j in range(SENT):

                @pl.when((s != me) if j == 0 else True)
                def _():
                    pltpu.make_async_remote_copy(
                        src_ref=blocks.at[0, 0],
                        dst_ref=held.at[s, j],
                        send_sem=out_sem.at[0, 0],
                        recv_sem=in_sem.at[s, j],
                        device_id=source(s, j),
                        device_id_type=MESH,
                    ).wait_recv()

            p_real, p_imag = patch(s)
            lit = []
            for m in range(modes):
                w_real = saved[s, m, 0].astype(jnp.float32)
                w_imag = saved[s, m, 1].astype(jnp.float32)
                lit.append(
                    (p_real * w_real - p_imag * w_imag, p_real * w_imag + p_imag * w_real)
                )
            moved = transform(tables.at[0], tables.at[1], lit, pixels)
            for m in range(modes):
                for part in range(2):
                    saved[s + 1, m, part] = moved[m][part].astype(jnp.bfloat16)

        last = [(saved[sections, m, 0], saved[sections, m, 1]) for m in range(modes)]
        far = transform(tables.at[2], tables.at[3], last, pixels)
        resid = -target[...]
        for real, imag in far:
            resid = resid + (real * real + imag * imag)
        seed = [(resid * real, resid * imag) for real, imag in far]
        seed = transform(tables.at[3], tables.at[2], seed, pixels)
        for m in range(modes):
            for part in range(2):
                back[m, part] = seed[m][part].astype(jnp.bfloat16)

        @pl.loop(0, sections)
        def _(step):
            s = sections - 1 - step
            p_real, p_imag = patch(s)
            waves = [(back[m, 0], back[m, 1]) for m in range(modes)]
            lit = transform(tables.at[1], tables.at[0], waves, pixels)
            g_real = jnp.zeros((pixels, pixels), jnp.float32)
            g_imag = jnp.zeros((pixels, pixels), jnp.float32)
            for m in range(modes):
                l_real, l_imag = lit[m]
                w_real = saved[s, m, 0].astype(jnp.float32)
                w_imag = saved[s, m, 1].astype(jnp.float32)
                g_real = g_real + (w_real * l_real + w_imag * l_imag)
                g_imag = g_imag + (w_real * l_imag - w_imag * l_real)
                back[m, 0] = (p_real * l_real + p_imag * l_imag).astype(jnp.bfloat16)
                back[m, 1] = (p_real * l_imag - p_imag * l_real).astype(jnp.bfloat16)
            mask = upper(window)
            for part, term in enumerate((g_real, g_imag)):
                top, bottom = term[:tile_rows], term[tile_rows:]
                made[s, 0, part] = jnp.where(mask, top, bottom).astype(made.dtype)
                made[s, 1, part] = jnp.where(mask, bottom, top).astype(made.dtype)
            for j in range(SENT):

                @pl.when((s != me) if j == 0 else True)
                def _():
                    term_out(s, j).start()

            @pl.when(s == me)
            def _():
                term_own().start()

        term_own().wait()

    def arrived(j, k):
        return pltpu.make_async_remote_copy(
            src_ref=made.at[0, 0],
            dst_ref=terms_ref.at[j, k],
            send_sem=made_sem.at[0, 0],
            recv_sem=terms_sem.at[j, k],
            device_id=worker_of(j, k, lat, lats, stride),
            device_id_type=MESH,
        )

    def pass_on(k):
        return pltpu.make_async_remote_copy(
            src_ref=terms_ref.at[0, k],
            dst_ref=terms_ref.at[2, k],
            send_sem=pass_sem.at[k],
            recv_sem=terms_sem.at[2, k],
            device_id=ahead,
            device_id_type=MESH,
        )

    upper_half = (2 * me) // sections

    def back_order(turn):
        return upper_half * (count - 1 - turn) + (1 - upper_half) * turn

    @pl.loop(0, count)
    def _(turn):
        k = back_order(turn)

        @pl.when(jnp.logical_not(mine(0, k)))
        def _():
            arrived(0, k).wait_recv()

        pass_on(k).start()

    @pl.when(works)
    def _():
        @pl.loop(0, sections)
        def _(s):
            for j in range(SENT):

                @pl.when((s != me) if j == 0 else True)
                def _():
                    term_out(s, j).wait_send()

    @pl.loop(0, count)
    def _(k):
        rows_out(k).wait_send()
        block_out(1, k).wait_send()
        arrived(1, k).wait_recv()
        pass_on(k).wait()

        @pl.when(jnp.logical_not(mine(0, k)))
        def _():
            block_out(0, k).wait_send()


def on_device(object_slices, probe, positions, measured):
    pixels = probe.shape[-1]
    tile_rows, cols = object_slices.shape[2:]
    count = positions.shape[0]
    sections = lax.axis_size("depth")
    lats = lax.axis_size("lat")
    low = jnp.bfloat16
    vmem = pl.BlockSpec(memory_space=pltpu.VMEM)
    smem = pl.BlockSpec(memory_space=pltpu.SMEM)
    anywhere = pl.BlockSpec(memory_space=pl.ANY)
    block = (2, tile_rows, pixels)
    tables = host_tables(pixels)
    near = [positions] + [shifted(positions, "lat", j) for j in range(1, TILES)]

    def extract(places):
        return pl.pallas_call(
            extract_kernel,
            out_shape=jax.ShapeDtypeStruct((len(places), count) + block, low),
            in_specs=[smem] * len(places) + [vmem],
            out_specs=vmem,
            compiler_params=pltpu.CompilerParams(vmem_limit_bytes=VMEM_BYTES),
            cost_estimate=pl.CostEstimate(
                flops=0, bytes_accessed=4 * object_slices[0].size, transcendentals=0
            ),
            name="extract",
        )(*places, object_slices)

    own_blocks = extract(near[:1])
    blocks = extract(near[1:])

    terms = pl.pallas_call(
        functools.partial(main_kernel, count, sections, lats),
        out_shape=jax.ShapeDtypeStruct((TILES, count) + block, low),
        in_specs=[smem, vmem, vmem] + [anywhere] * 3,
        out_specs=anywhere,
        scratch_shapes=[
            pltpu.VMEM((count,) + block, low),
            pltpu.VMEM((count,) + block, low),
            pltpu.VMEM((sections, SENT) + block, low),
            pltpu.VMEM((sections, SENT) + block, low),
            pltpu.VMEM((sections + 1,) + probe.shape, low),
            pltpu.VMEM(probe.shape, low),
            pltpu.VMEM(tables.shape, low),
            pltpu.VMEM(probe.shape, jnp.float32),
            pltpu.VMEM(measured.shape[1:], jnp.float32),
            pltpu.SemaphoreType.DMA((3,)),
            pltpu.SemaphoreType.DMA((SENT, count)),
            pltpu.SemaphoreType.DMA((sections, SENT)),
            pltpu.SemaphoreType.DMA((2,)),
            pltpu.SemaphoreType.DMA((sections, SENT)),
            pltpu.SemaphoreType.DMA((TILES, count)),
            pltpu.SemaphoreType.DMA((count,)),
            pltpu.SemaphoreType.DMA((count,)),
            pltpu.SemaphoreType.DMA((count,)),
        ],
        compiler_params=pltpu.CompilerParams(
            collective_id=0, has_side_effects=True, vmem_limit_bytes=VMEM_BYTES
        ),
        name="windows",
    )(positions, own_blocks, blocks, probe, measured, tables)

    return pl.pallas_call(
        gather_kernel,
        out_shape=jax.ShapeDtypeStruct(object_slices.shape, jnp.float32),
        in_specs=[smem] * TILES + [vmem],
        out_specs=vmem,
        compiler_params=pltpu.CompilerParams(vmem_limit_bytes=VMEM_BYTES),
        name="gather",
    )(*near, terms)


def solution(mesh):
    return jax.shard_map(
        on_device,
        mesh=mesh,
        in_specs=(P("depth", None, "lat", None), P(), P("lat", None), P("lat", None, None)),
        out_specs=P("depth", None, "lat", None),
        check_vma=False,
    )
```

```python
import functools
import math

import jax
import jax.numpy as jnp
import ml_dtypes
import numpy as np
from jax import lax
from jax.experimental import pallas as pl
from jax.experimental.pallas import tpu as pltpu
from jax.sharding import PartitionSpec as P

fresnel = 0.5
MESH = pl.DeviceIdType.MESH
TILES = 3
SENT = 2
LANES = 128
VMEM_BYTES = 48 * 1024 * 1024


def shifted(block, axis, distance):
    devices = range(lax.axis_size(axis))
    route = [((i - distance) % len(devices), i) for i in devices]
    return lax.ppermute(block, axis, route)


def host_tables(pixels):
    idx = np.arange(pixels)
    angle = 2.0 * np.pi * (np.outer(idx, idx) % pixels) / pixels
    far = np.exp(-1j * angle) / math.sqrt(pixels)
    freq = np.where(idx < pixels // 2, idx, idx - pixels).astype(np.float64)
    prop = (np.conj(far) * np.exp(-1j * np.pi * fresnel * freq * freq / pixels)[None, :]) @ far

    def block(table):
        return np.block([[table.real, -table.imag], [table.imag, table.real]])

    prop_block, far_block = block(prop), block(far)
    tables = np.stack([prop_block, prop_block.T, far_block, far_block.T])
    high = tables.astype(ml_dtypes.bfloat16)
    rest = (tables - high.astype(np.float64)).astype(ml_dtypes.bfloat16)
    return jnp.asarray(np.stack([high, rest], axis=1))


def window_place(positions_ref, k, tile_rows, col_tiles):
    row = lax.rem(positions_ref[k, 0], tile_rows)
    col = positions_ref[k, 1]
    first = jnp.minimum(col // LANES, col_tiles - 3)
    return row, first, col - first * LANES


def upper_rows(shape, keep):
    return lax.broadcasted_iota(jnp.int32, shape, 0) < keep


def extract_kernel(*refs):
    *near, tile_ref, blocks_ref = refs
    _, _, tile_rows, cols = tile_ref.shape
    _, count, _, _, pixels = blocks_ref.shape
    wide = pixels + LANES

    for j in range(len(near)):

        @pl.loop(0, count)
        def _(k):
            row, first, shift = window_place(near[j], k, tile_rows, cols // LANES)
            start = pl.multiple_of(first * LANES, LANES)
            for part in range(2):
                piece = tile_ref[0, part, :, pl.ds(start, wide)]
                piece = pltpu.roll(piece, lax.rem(wide - shift, wide), 1)[:, :pixels]
                piece = pltpu.roll(piece, lax.rem(tile_rows - row, tile_rows), 0)
                blocks_ref[j, k, part] = piece.astype(blocks_ref.dtype)


def gather_kernel(near0_ref, near1_ref, near2_ref, terms_ref, grad_ref):
    near = (near0_ref, near1_ref, near2_ref)
    _, _, tile_rows, cols = grad_ref.shape
    _, count, _, _, pixels = terms_ref.shape
    wide = pixels + LANES
    grad_ref[...] = jnp.zeros_like(grad_ref)

    for j in range(TILES):

        @pl.loop(0, count)
        def _(k):
            row, first, shift = window_place(near[j], k, tile_rows, cols // LANES)
            start = pl.multiple_of(first * LANES, LANES)
            for part in range(2):
                piece = terms_ref[j, k, part].astype(jnp.float32)
                if j != 1:
                    upper = upper_rows(piece.shape, tile_rows - row)
                    kept = upper if j == 0 else jnp.logical_not(upper)
                    piece = jnp.where(kept, piece, 0.0)
                piece = pltpu.roll(piece, row, 0)
                piece = jnp.concatenate(
                    [piece, jnp.zeros((tile_rows, LANES), jnp.float32)], axis=1
                )
                piece = pltpu.roll(piece, shift, 1)
                grad_ref[0, part, :, pl.ds(start, wide)] += piece


def spread(count, sections, lats):
    stride = sections // count
    me = lax.axis_index("depth")
    lat = lax.axis_index("lat")
    works = (lax.rem(me, stride) == lax.rem(lat, stride)) & (me // stride < count)
    return stride, me, lat, works


def worker_of(j, k, lat, lats, stride):
    owner = lax.rem(lat - j + lats, lats)
    return {"depth": k * stride + lax.rem(owner, stride), "lat": owner}


def transform(left, right, parts, pixels):
    low = jnp.bfloat16
    stacked = jnp.concatenate(
        [jnp.concatenate([p.astype(low) for p in pair], axis=0) for pair in parts], axis=1
    )
    dot = functools.partial(jnp.dot, preferred_element_type=jnp.float32)
    middle = (dot(left[0], stacked) + dot(left[1], stacked)).astype(low)
    rows = [
        jnp.concatenate(
            [
                middle[:pixels, m * pixels : (m + 1) * pixels],
                middle[pixels:, m * pixels : (m + 1) * pixels],
            ],
            axis=1,
        )
        for m in range(len(parts))
    ]
    joined = jnp.concatenate(rows, axis=0)
    ended = dot(joined, right[0]) + dot(joined, right[1])
    return [
        (
            ended[m * pixels : (m + 1) * pixels, :pixels],
            ended[m * pixels : (m + 1) * pixels, pixels:],
        )
        for m in range(len(parts))
    ]


def main_kernel(
    count,
    sections,
    lats,
    near0_ref,
    own_blocks,
    blocks,
    probe_ref,
    measured_ref,
    tables_ref,
    terms_ref,
    merged,
    halo,
    held,
    made,
    saved,
    back,
    tables,
    start_wave,
    target,
    load_sem,
    out_sem,
    in_sem,
    own_sem,
    made_sem,
    terms_sem,
    halo_out_sem,
    halo_in_sem,
    pass_sem,
):
    tile_rows, pixels = held.shape[3:]
    modes = probe_ref.shape[0]
    stride, me, lat, works = spread(count, sections, lats)
    window = lax.rem(me // stride, count)

    def source(s, j):
        return {"depth": s, "lat": lax.rem(lat + j, lats)}

    def mine(j, k):
        return works & (window == k) if j == 0 else False

    barrier = pltpu.get_barrier_semaphore()
    for j in range(SENT):

        @pl.loop(0, count)
        def _(k):
            @pl.when(jnp.logical_not(mine(j, k)))
            def _():
                pl.semaphore_signal(
                    barrier,
                    inc=1,
                    device_id=worker_of(j, k, lat, lats, stride),
                    device_id_type=MESH,
                )

    ahead = {"depth": me, "lat": lax.rem(lat + 2, lats)}
    behind = {"depth": me, "lat": lax.rem(lat - 2 + lats, lats)}
    for peer in (ahead, behind):
        pl.semaphore_signal(barrier, inc=1, device_id=peer, device_id_type=MESH)

    loads = (
        pltpu.make_async_copy(tables_ref, tables, load_sem.at[0]),
        pltpu.make_async_copy(probe_ref, start_wave, load_sem.at[1]),
        pltpu.make_async_copy(measured_ref.at[window], target, load_sem.at[2]),
    )

    @pl.when(works)
    def _():
        for j in range(SENT):

            @pl.loop(0, sections)
            def _(s):
                @pl.when((s != me) if j == 0 else True)
                def _():
                    pl.semaphore_signal(
                        barrier, inc=1, device_id=source(s, j), device_id_type=MESH
                    )

        for load in loads:
            load.start()

    busy = works.astype(jnp.int32)
    pl.semaphore_wait(barrier, SENT * count + 2 - busy + busy * (SENT * sections - 1))

    def block_out(j, k):
        return pltpu.make_async_remote_copy(
            src_ref=merged.at[k] if j == 0 else blocks.at[j - 1, k],
            dst_ref=held.at[me, j],
            send_sem=out_sem.at[j, k],
            recv_sem=in_sem.at[me, j],
            device_id=worker_of(j, k, lat, lats, stride),
            device_id_type=MESH,
        )

    def block_own(k):
        return pltpu.make_async_copy(merged.at[k], held.at[me, 0], own_sem.at[0])

    far_first = 1 - jnp.minimum((4 * me) // sections, 1)

    def order(turn):
        return far_first * (count - 1 - turn) + (1 - far_first) * turn

    def rows_out(k):
        return pltpu.make_async_remote_copy(
            src_ref=blocks.at[1, k],
            dst_ref=halo.at[k],
            send_sem=halo_out_sem.at[k],
            recv_sem=halo_in_sem.at[k],
            device_id=behind,
            device_id_type=MESH,
        )

    @pl.loop(0, count)
    def _(turn):
        rows_out(order(turn)).start()

    def upper(k):
        keep = tile_rows - lax.rem(near0_ref[k, 0], tile_rows)
        return upper_rows((tile_rows, pixels), keep)

    def merge_and_send(turn):
        k = order(turn)
        rows_out(k).wait_recv()
        for part in range(2):
            merged[k, part] = jnp.where(
                upper(k),
                own_blocks[0, k, part].astype(jnp.float32),
                halo[k, part].astype(jnp.float32),
            ).astype(merged.dtype)
        own = mine(0, k)

        @pl.when(own)
        def _():
            block_own(k).start()

        @pl.when(jnp.logical_not(own))
        def _():
            block_out(0, k).start()

    half = (count + 1) // 2
    for begin, end in ((0, half), (half, count)):

        @pl.loop(begin, end)
        def _(turn):
            block_out(1, order(turn)).start()

        pl.loop(begin, end)(merge_and_send)

    def term_out(s, j):
        return pltpu.make_async_remote_copy(
            src_ref=made.at[s, j],
            dst_ref=terms_ref.at[j, window],
            send_sem=made_sem.at[s, j],
            recv_sem=terms_sem.at[j, window],
            device_id=source(s, j),
            device_id_type=MESH,
        )

    def term_own():
        return pltpu.make_async_copy(
            made.at[me, 0], terms_ref.at[0, window], own_sem.at[1]
        )

    def patch(s):
        mask = upper(window)
        out = []
        for part in range(2):
            a, b = (held[s, j, part].astype(jnp.float32) for j in range(SENT))
            out.append(
                jnp.concatenate([jnp.where(mask, a, b), jnp.where(mask, b, a)], axis=0)
            )
        return out

    @pl.when(works)
    def _():
        for load in loads:
            load.wait()
        saved[0] = start_wave[...].astype(jnp.bfloat16)
        block_own(window).wait()

        @pl.loop(0, sections)
        def _(s):
            for j in range(SENT):

                @pl.when((s != me) if j == 0 else True)
                def _():
                    pltpu.make_async_remote_copy(
                        src_ref=blocks.at[0, 0],
                        dst_ref=held.at[s, j],
                        send_sem=out_sem.at[0, 0],
                        recv_sem=in_sem.at[s, j],
                        device_id=source(s, j),
                        device_id_type=MESH,
                    ).wait_recv()

            p_real, p_imag = patch(s)
            lit = []
            for m in range(modes):
                w_real = saved[s, m, 0].astype(jnp.float32)
                w_imag = saved[s, m, 1].astype(jnp.float32)
                lit.append(
                    (p_real * w_real - p_imag * w_imag, p_real * w_imag + p_imag * w_real)
                )
            moved = transform(tables.at[0], tables.at[1], lit, pixels)
            for m in range(modes):
                for part in range(2):
                    saved[s + 1, m, part] = moved[m][part].astype(jnp.bfloat16)

        last = [(saved[sections, m, 0], saved[sections, m, 1]) for m in range(modes)]
        far = transform(tables.at[2], tables.at[3], last, pixels)
        resid = -target[...]
        for real, imag in far:
            resid = resid + (real * real + imag * imag)
        seed = [(resid * real, resid * imag) for real, imag in far]
        seed = transform(tables.at[3], tables.at[2], seed, pixels)
        for m in range(modes):
            for part in range(2):
                back[m, part] = seed[m][part].astype(jnp.bfloat16)

        @pl.loop(0, sections)
        def _(step):
            s = sections - 1 - step
            p_real, p_imag = patch(s)
            waves = [(back[m, 0], back[m, 1]) for m in range(modes)]
            lit = transform(tables.at[1], tables.at[0], waves, pixels)
            g_real = jnp.zeros((pixels, pixels), jnp.float32)
            g_imag = jnp.zeros((pixels, pixels), jnp.float32)
            for m in range(modes):
                l_real, l_imag = lit[m]
                w_real = saved[s, m, 0].astype(jnp.float32)
                w_imag = saved[s, m, 1].astype(jnp.float32)
                g_real = g_real + (w_real * l_real + w_imag * l_imag)
                g_imag = g_imag + (w_real * l_imag - w_imag * l_real)
                back[m, 0] = (p_real * l_real + p_imag * l_imag).astype(jnp.bfloat16)
                back[m, 1] = (p_real * l_imag - p_imag * l_real).astype(jnp.bfloat16)
            mask = upper(window)
            for part, term in enumerate((g_real, g_imag)):
                top, bottom = term[:tile_rows], term[tile_rows:]
                made[s, 0, part] = jnp.where(mask, top, bottom).astype(made.dtype)
                made[s, 1, part] = jnp.where(mask, bottom, top).astype(made.dtype)
            for j in range(SENT):

                @pl.when((s != me) if j == 0 else True)
                def _():
                    term_out(s, j).start()

            @pl.when(s == me)
            def _():
                term_own().start()

        term_own().wait()

    def arrived(j, k):
        return pltpu.make_async_remote_copy(
            src_ref=made.at[0, 0],
            dst_ref=terms_ref.at[j, k],
            send_sem=made_sem.at[0, 0],
            recv_sem=terms_sem.at[j, k],
            device_id=worker_of(j, k, lat, lats, stride),
            device_id_type=MESH,
        )

    def pass_on(k):
        return pltpu.make_async_remote_copy(
            src_ref=terms_ref.at[0, k],
            dst_ref=terms_ref.at[2, k],
            send_sem=pass_sem.at[k],
            recv_sem=terms_sem.at[2, k],
            device_id=ahead,
            device_id_type=MESH,
        )

    upper_half = (2 * me) // sections

    def back_order(turn):
        return upper_half * (count - 1 - turn) + (1 - upper_half) * turn

    @pl.loop(0, count)
    def _(turn):
        k = back_order(turn)

        @pl.when(jnp.logical_not(mine(0, k)))
        def _():
            arrived(0, k).wait_recv()

        pass_on(k).start()

    @pl.when(works)
    def _():
        @pl.loop(0, sections)
        def _(s):
            for j in range(SENT):

                @pl.when((s != me) if j == 0 else True)
                def _():
                    term_out(s, j).wait_send()

    @pl.loop(0, count)
    def _(k):
        rows_out(k).wait_send()
        block_out(1, k).wait_send()
        arrived(1, k).wait_recv()
        pass_on(k).wait()

        @pl.when(jnp.logical_not(mine(0, k)))
        def _():
            block_out(0, k).wait_send()


def on_device(object_slices, probe, positions, measured):
    pixels = probe.shape[-1]
    tile_rows, cols = object_slices.shape[2:]
    count = positions.shape[0]
    sections = lax.axis_size("depth")
    lats = lax.axis_size("lat")
    low = jnp.bfloat16
    vmem = pl.BlockSpec(memory_space=pltpu.VMEM)
    smem = pl.BlockSpec(memory_space=pltpu.SMEM)
    anywhere = pl.BlockSpec(memory_space=pl.ANY)
    block = (2, tile_rows, pixels)
    tables = host_tables(pixels)
    near = [positions] + [shifted(positions, "lat", j) for j in range(1, TILES)]

    def extract(places):
        return pl.pallas_call(
            extract_kernel,
            out_shape=jax.ShapeDtypeStruct((len(places), count) + block, low),
            in_specs=[smem] * len(places) + [vmem],
            out_specs=vmem,
            compiler_params=pltpu.CompilerParams(vmem_limit_bytes=VMEM_BYTES),
            cost_estimate=pl.CostEstimate(
                flops=0, bytes_accessed=4 * object_slices[0].size, transcendentals=0
            ),
            name="extract",
        )(*places, object_slices)

    own_blocks = extract(near[:1])
    blocks = extract(near[1:])

    terms = pl.pallas_call(
        functools.partial(main_kernel, count, sections, lats),
        out_shape=jax.ShapeDtypeStruct((TILES, count) + block, low),
        in_specs=[smem, vmem, vmem] + [anywhere] * 3,
        out_specs=anywhere,
        scratch_shapes=[
            pltpu.VMEM((count,) + block, low),
            pltpu.VMEM((count,) + block, low),
            pltpu.VMEM((sections, SENT) + block, low),
            pltpu.VMEM((sections, SENT) + block, low),
            pltpu.VMEM((sections + 1,) + probe.shape, low),
            pltpu.VMEM(probe.shape, low),
            pltpu.VMEM(tables.shape, low),
            pltpu.VMEM(probe.shape, jnp.float32),
            pltpu.VMEM(measured.shape[1:], jnp.float32),
            pltpu.SemaphoreType.DMA((3,)),
            pltpu.SemaphoreType.DMA((SENT, count)),
            pltpu.SemaphoreType.DMA((sections, SENT)),
            pltpu.SemaphoreType.DMA((2,)),
            pltpu.SemaphoreType.DMA((sections, SENT)),
            pltpu.SemaphoreType.DMA((TILES, count)),
            pltpu.SemaphoreType.DMA((count,)),
            pltpu.SemaphoreType.DMA((count,)),
            pltpu.SemaphoreType.DMA((count,)),
        ],
        compiler_params=pltpu.CompilerParams(
            collective_id=0, has_side_effects=True, vmem_limit_bytes=VMEM_BYTES
        ),
        name="windows",
    )(positions, own_blocks, blocks, probe, measured, tables)

    return pl.pallas_call(
        gather_kernel,
        out_shape=jax.ShapeDtypeStruct(object_slices.shape, jnp.float32),
        in_specs=[smem] * TILES + [vmem],
        out_specs=vmem,
        compiler_params=pltpu.CompilerParams(vmem_limit_bytes=VMEM_BYTES),
        name="gather",
    )(*near, terms)


def solution(mesh):
    return jax.shard_map(
        on_device,
        mesh=mesh,
        in_specs=(P("depth", None, "lat", None), P(), P("lat", None), P("lat", None, None)),
        out_specs=P("depth", None, "lat", None),
        check_vma=False,
    )
```

```python
import functools
import math

import jax
import jax.numpy as jnp
import ml_dtypes
import numpy as np
from jax import lax
from jax.experimental import pallas as pl
from jax.experimental.pallas import tpu as pltpu
from jax.sharding import PartitionSpec as P

fresnel = 0.5
MESH = pl.DeviceIdType.MESH
TILES = 3
SENT = 2
LANES = 128
VMEM_BYTES = 48 * 1024 * 1024


def shifted(block, axis, distance):
    devices = range(lax.axis_size(axis))
    route = [((i - distance) % len(devices), i) for i in devices]
    return lax.ppermute(block, axis, route)


def host_tables(pixels):
    idx = np.arange(pixels)
    angle = 2.0 * np.pi * (np.outer(idx, idx) % pixels) / pixels
    far = np.exp(-1j * angle) / math.sqrt(pixels)
    freq = np.where(idx < pixels // 2, idx, idx - pixels).astype(np.float64)
    prop = (np.conj(far) * np.exp(-1j * np.pi * fresnel * freq * freq / pixels)[None, :]) @ far

    def block(table):
        return np.block([[table.real, -table.imag], [table.imag, table.real]])

    prop_block, far_block = block(prop), block(far)
    tables = np.stack([prop_block, prop_block.T, far_block, far_block.T])
    high = tables.astype(ml_dtypes.bfloat16)
    rest = (tables - high.astype(np.float64)).astype(ml_dtypes.bfloat16)
    return jnp.asarray(np.stack([high, rest], axis=1))


def window_place(positions_ref, k, tile_rows, col_tiles):
    row = lax.rem(positions_ref[k, 0], tile_rows)
    col = positions_ref[k, 1]
    first = jnp.minimum(col // LANES, col_tiles - 3)
    return row, first, col - first * LANES


def upper_rows(shape, keep):
    return lax.broadcasted_iota(jnp.int32, shape, 0) < keep


def extract_kernel(*refs):
    *near, tile_ref, blocks_ref = refs
    _, _, tile_rows, cols = tile_ref.shape
    _, count, _, _, pixels = blocks_ref.shape
    wide = pixels + LANES

    for j in range(len(near)):

        @pl.loop(0, count, unroll=True)
        def _(k):
            row, first, shift = window_place(near[j], k, tile_rows, cols // LANES)
            start = pl.multiple_of(first * LANES, LANES)
            for part in range(2):
                piece = tile_ref[0, part, :, pl.ds(start, wide)]
                piece = pltpu.roll(piece, lax.rem(wide - shift, wide), 1)[:, :pixels]
                piece = pltpu.roll(piece, lax.rem(tile_rows - row, tile_rows), 0)
                blocks_ref[j, k, part] = piece.astype(blocks_ref.dtype)


def gather_kernel(near0_ref, near1_ref, near2_ref, terms_ref, grad_ref):
    near = (near0_ref, near1_ref, near2_ref)
    _, _, tile_rows, cols = grad_ref.shape
    _, count, _, _, pixels = terms_ref.shape
    wide = pixels + LANES
    grad_ref[...] = jnp.zeros_like(grad_ref)

    for j in range(TILES):

        @pl.loop(0, count, unroll=True)
        def _(k):
            row, first, shift = window_place(near[j], k, tile_rows, cols // LANES)
            start = pl.multiple_of(first * LANES, LANES)
            for part in range(2):
                piece = terms_ref[j, k, part].astype(jnp.float32)
                if j != 1:
                    upper = upper_rows(piece.shape, tile_rows - row)
                    kept = upper if j == 0 else jnp.logical_not(upper)
                    piece = jnp.where(kept, piece, 0.0)
                piece = pltpu.roll(piece, row, 0)
                piece = jnp.concatenate(
                    [piece, jnp.zeros((tile_rows, LANES), jnp.float32)], axis=1
                )
                piece = pltpu.roll(piece, shift, 1)
                grad_ref[0, part, :, pl.ds(start, wide)] += piece


def spread(count, sections, lats):
    stride = sections // count
    me = lax.axis_index("depth")
    lat = lax.axis_index("lat")
    works = (lax.rem(me, stride) == lax.rem(lat, stride)) & (me // stride < count)
    return stride, me, lat, works


def worker_of(j, k, lat, lats, stride):
    owner = lax.rem(lat - j + lats, lats)
    return {"depth": k * stride + lax.rem(owner, stride), "lat": owner}


def transform(left, right, parts, pixels):
    low = jnp.bfloat16
    stacked = jnp.concatenate(
        [jnp.concatenate([p.astype(low) for p in pair], axis=0) for pair in parts], axis=1
    )
    dot = functools.partial(jnp.dot, preferred_element_type=jnp.float32)
    middle = (dot(left[0], stacked) + dot(left[1], stacked)).astype(low)
    rows = [
        jnp.concatenate(
            [
                middle[:pixels, m * pixels : (m + 1) * pixels],
                middle[pixels:, m * pixels : (m + 1) * pixels],
            ],
            axis=1,
        )
        for m in range(len(parts))
    ]
    joined = jnp.concatenate(rows, axis=0)
    ended = dot(joined, right[0]) + dot(joined, right[1])
    return [
        (
            ended[m * pixels : (m + 1) * pixels, :pixels],
            ended[m * pixels : (m + 1) * pixels, pixels:],
        )
        for m in range(len(parts))
    ]


def main_kernel(
    count,
    sections,
    lats,
    near0_ref,
    own_blocks,
    blocks,
    probe_ref,
    measured_ref,
    tables_ref,
    terms_ref,
    merged,
    halo,
    held,
    made,
    saved,
    back,
    tables,
    start_wave,
    target,
    load_sem,
    out_sem,
    in_sem,
    own_sem,
    made_sem,
    terms_sem,
    halo_out_sem,
    halo_in_sem,
    pass_sem,
):
    tile_rows, pixels = held.shape[3:]
    modes = probe_ref.shape[0]
    stride, me, lat, works = spread(count, sections, lats)
    window = lax.rem(me // stride, count)

    def source(s, j):
        return {"depth": s, "lat": lax.rem(lat + j, lats)}

    def mine(j, k):
        return works & (window == k) if j == 0 else False

    barrier = pltpu.get_barrier_semaphore()
    for j in range(SENT):

        @pl.loop(0, count)
        def _(k):
            @pl.when(jnp.logical_not(mine(j, k)))
            def _():
                pl.semaphore_signal(
                    barrier,
                    inc=1,
                    device_id=worker_of(j, k, lat, lats, stride),
                    device_id_type=MESH,
                )

    ahead = {"depth": me, "lat": lax.rem(lat + 2, lats)}
    behind = {"depth": me, "lat": lax.rem(lat - 2 + lats, lats)}
    for peer in (ahead, behind):
        pl.semaphore_signal(barrier, inc=1, device_id=peer, device_id_type=MESH)

    loads = (
        pltpu.make_async_copy(tables_ref, tables, load_sem.at[0]),
        pltpu.make_async_copy(probe_ref, start_wave, load_sem.at[1]),
        pltpu.make_async_copy(measured_ref.at[window], target, load_sem.at[2]),
    )

    @pl.when(works)
    def _():
        for j in range(SENT):

            @pl.loop(0, sections)
            def _(s):
                @pl.when((s != me) if j == 0 else True)
                def _():
                    pl.semaphore_signal(
                        barrier, inc=1, device_id=source(s, j), device_id_type=MESH
                    )

        for load in loads:
            load.start()

    busy = works.astype(jnp.int32)
    pl.semaphore_wait(barrier, SENT * count + 2 - busy + busy * (SENT * sections - 1))

    def block_out(j, k):
        return pltpu.make_async_remote_copy(
            src_ref=merged.at[k] if j == 0 else blocks.at[j - 1, k],
            dst_ref=held.at[me, j],
            send_sem=out_sem.at[j, k],
            recv_sem=in_sem.at[me, j],
            device_id=worker_of(j, k, lat, lats, stride),
            device_id_type=MESH,
        )

    def block_own(k):
        return pltpu.make_async_copy(merged.at[k], held.at[me, 0], own_sem.at[0])

    far_first = 1 - jnp.minimum((4 * me) // sections, 1)

    def order(turn):
        return far_first * (count - 1 - turn) + (1 - far_first) * turn

    def rows_out(k):
        return pltpu.make_async_remote_copy(
            src_ref=blocks.at[1, k],
            dst_ref=halo.at[k],
            send_sem=halo_out_sem.at[k],
            recv_sem=halo_in_sem.at[k],
            device_id=behind,
            device_id_type=MESH,
        )

    @pl.loop(0, count)
    def _(turn):
        rows_out(order(turn)).start()

    @pl.loop(0, count)
    def _(turn):
        block_out(1, order(turn)).start()

    def upper(k):
        keep = tile_rows - lax.rem(near0_ref[k, 0], tile_rows)
        return upper_rows((tile_rows, pixels), keep)

    @pl.loop(0, count)
    def _(turn):
        k = order(turn)
        rows_out(k).wait_recv()
        for part in range(2):
            merged[k, part] = jnp.where(
                upper(k),
                own_blocks[0, k, part].astype(jnp.float32),
                halo[k, part].astype(jnp.float32),
            ).astype(merged.dtype)
        own = mine(0, k)

        @pl.when(own)
        def _():
            block_own(k).start()

        @pl.when(jnp.logical_not(own))
        def _():
            block_out(0, k).start()

    def term_out(s, j):
        return pltpu.make_async_remote_copy(
            src_ref=made.at[s, j],
            dst_ref=terms_ref.at[j, window],
            send_sem=made_sem.at[s, j],
            recv_sem=terms_sem.at[j, window],
            device_id=source(s, j),
            device_id_type=MESH,
        )

    def term_own():
        return pltpu.make_async_copy(
            made.at[me, 0], terms_ref.at[0, window], own_sem.at[1]
        )

    def patch(s):
        mask = upper(window)
        out = []
        for part in range(2):
            a, b = (held[s, j, part].astype(jnp.float32) for j in range(SENT))
            out.append(
                jnp.concatenate([jnp.where(mask, a, b), jnp.where(mask, b, a)], axis=0)
            )
        return out

    @pl.when(works)
    def _():
        for load in loads:
            load.wait()
        saved[0] = start_wave[...].astype(jnp.bfloat16)
        block_own(window).wait()

        @pl.loop(0, sections)
        def _(s):
            for j in range(SENT):

                @pl.when((s != me) if j == 0 else True)
                def _():
                    pltpu.make_async_remote_copy(
                        src_ref=blocks.at[0, 0],
                        dst_ref=held.at[s, j],
                        send_sem=out_sem.at[0, 0],
                        recv_sem=in_sem.at[s, j],
                        device_id=source(s, j),
                        device_id_type=MESH,
                    ).wait_recv()

            p_real, p_imag = patch(s)
            lit = []
            for m in range(modes):
                w_real = saved[s, m, 0].astype(jnp.float32)
                w_imag = saved[s, m, 1].astype(jnp.float32)
                lit.append(
                    (p_real * w_real - p_imag * w_imag, p_real * w_imag + p_imag * w_real)
                )
            moved = transform(tables.at[0], tables.at[1], lit, pixels)
            for m in range(modes):
                for part in range(2):
                    saved[s + 1, m, part] = moved[m][part].astype(jnp.bfloat16)

        last = [(saved[sections, m, 0], saved[sections, m, 1]) for m in range(modes)]
        far = transform(tables.at[2], tables.at[3], last, pixels)
        resid = -target[...]
        for real, imag in far:
            resid = resid + (real * real + imag * imag)
        seed = [(resid * real, resid * imag) for real, imag in far]
        seed = transform(tables.at[3], tables.at[2], seed, pixels)
        for m in range(modes):
            for part in range(2):
                back[m, part] = seed[m][part].astype(jnp.bfloat16)

        @pl.loop(0, sections)
        def _(step):
            s = sections - 1 - step
            p_real, p_imag = patch(s)
            waves = [(back[m, 0], back[m, 1]) for m in range(modes)]
            lit = transform(tables.at[1], tables.at[0], waves, pixels)
            g_real = jnp.zeros((pixels, pixels), jnp.float32)
            g_imag = jnp.zeros((pixels, pixels), jnp.float32)
            for m in range(modes):
                l_real, l_imag = lit[m]
                w_real = saved[s, m, 0].astype(jnp.float32)
                w_imag = saved[s, m, 1].astype(jnp.float32)
                g_real = g_real + (w_real * l_real + w_imag * l_imag)
                g_imag = g_imag + (w_real * l_imag - w_imag * l_real)
                back[m, 0] = (p_real * l_real + p_imag * l_imag).astype(jnp.bfloat16)
                back[m, 1] = (p_real * l_imag - p_imag * l_real).astype(jnp.bfloat16)
            mask = upper(window)
            for part, term in enumerate((g_real, g_imag)):
                top, bottom = term[:tile_rows], term[tile_rows:]
                made[s, 0, part] = jnp.where(mask, top, bottom).astype(made.dtype)
                made[s, 1, part] = jnp.where(mask, bottom, top).astype(made.dtype)
            for j in range(SENT):

                @pl.when((s != me) if j == 0 else True)
                def _():
                    term_out(s, j).start()

            @pl.when(s == me)
            def _():
                term_own().start()

        term_own().wait()

    def arrived(j, k):
        return pltpu.make_async_remote_copy(
            src_ref=made.at[0, 0],
            dst_ref=terms_ref.at[j, k],
            send_sem=made_sem.at[0, 0],
            recv_sem=terms_sem.at[j, k],
            device_id=worker_of(j, k, lat, lats, stride),
            device_id_type=MESH,
        )

    def pass_on(k):
        return pltpu.make_async_remote_copy(
            src_ref=terms_ref.at[0, k],
            dst_ref=terms_ref.at[2, k],
            send_sem=pass_sem.at[k],
            recv_sem=terms_sem.at[2, k],
            device_id=ahead,
            device_id_type=MESH,
        )

    upper_half = (2 * me) // sections

    def back_order(turn):
        return upper_half * (count - 1 - turn) + (1 - upper_half) * turn

    @pl.loop(0, count)
    def _(turn):
        k = back_order(turn)

        @pl.when(jnp.logical_not(mine(0, k)))
        def _():
            arrived(0, k).wait_recv()

        pass_on(k).start()

    @pl.when(works)
    def _():
        @pl.loop(0, sections)
        def _(s):
            for j in range(SENT):

                @pl.when((s != me) if j == 0 else True)
                def _():
                    term_out(s, j).wait_send()

    @pl.loop(0, count)
    def _(k):
        rows_out(k).wait_send()
        block_out(1, k).wait_send()
        arrived(1, k).wait_recv()
        pass_on(k).wait()

        @pl.when(jnp.logical_not(mine(0, k)))
        def _():
            block_out(0, k).wait_send()


def on_device(object_slices, probe, positions, measured):
    pixels = probe.shape[-1]
    tile_rows, cols = object_slices.shape[2:]
    count = positions.shape[0]
    sections = lax.axis_size("depth")
    lats = lax.axis_size("lat")
    low = jnp.bfloat16
    vmem = pl.BlockSpec(memory_space=pltpu.VMEM)
    smem = pl.BlockSpec(memory_space=pltpu.SMEM)
    anywhere = pl.BlockSpec(memory_space=pl.ANY)
    block = (2, tile_rows, pixels)
    tables = host_tables(pixels)
    near = [positions] + [shifted(positions, "lat", j) for j in range(1, TILES)]

    def extract(places):
        return pl.pallas_call(
            extract_kernel,
            out_shape=jax.ShapeDtypeStruct((len(places), count) + block, low),
            in_specs=[smem] * len(places) + [vmem],
            out_specs=vmem,
            compiler_params=pltpu.CompilerParams(vmem_limit_bytes=VMEM_BYTES),
            cost_estimate=pl.CostEstimate(
                flops=0, bytes_accessed=4 * object_slices[0].size, transcendentals=0
            ),
            name="extract",
        )(*places, object_slices)

    own_blocks = extract(near[:1])
    blocks = extract(near[1:])

    terms = pl.pallas_call(
        functools.partial(main_kernel, count, sections, lats),
        out_shape=jax.ShapeDtypeStruct((TILES, count) + block, low),
        in_specs=[smem, vmem, vmem] + [anywhere] * 3,
        out_specs=anywhere,
        scratch_shapes=[
            pltpu.VMEM((count,) + block, low),
            pltpu.VMEM((count,) + block, low),
            pltpu.VMEM((sections, SENT) + block, low),
            pltpu.VMEM((sections, SENT) + block, low),
            pltpu.VMEM((sections + 1,) + probe.shape, low),
            pltpu.VMEM(probe.shape, low),
            pltpu.VMEM(tables.shape, low),
            pltpu.VMEM(probe.shape, jnp.float32),
            pltpu.VMEM(measured.shape[1:], jnp.float32),
            pltpu.SemaphoreType.DMA((3,)),
            pltpu.SemaphoreType.DMA((SENT, count)),
            pltpu.SemaphoreType.DMA((sections, SENT)),
            pltpu.SemaphoreType.DMA((2,)),
            pltpu.SemaphoreType.DMA((sections, SENT)),
            pltpu.SemaphoreType.DMA((TILES, count)),
            pltpu.SemaphoreType.DMA((count,)),
            pltpu.SemaphoreType.DMA((count,)),
            pltpu.SemaphoreType.DMA((count,)),
        ],
        compiler_params=pltpu.CompilerParams(
            collective_id=0, has_side_effects=True, vmem_limit_bytes=VMEM_BYTES
        ),
        name="windows",
    )(positions, own_blocks, blocks, probe, measured, tables)

    return pl.pallas_call(
        gather_kernel,
        out_shape=jax.ShapeDtypeStruct(object_slices.shape, jnp.float32),
        in_specs=[smem] * TILES + [vmem],
        out_specs=vmem,
        compiler_params=pltpu.CompilerParams(vmem_limit_bytes=VMEM_BYTES),
        name="gather",
    )(*near, terms)


def solution(mesh):
    return jax.shard_map(
        on_device,
        mesh=mesh,
        in_specs=(P("depth", None, "lat", None), P(), P("lat", None), P("lat", None, None)),
        out_specs=P("depth", None, "lat", None),
        check_vma=False,
    )
```
